512 devices in a mesh: role: 4 (over y_lo, core), shard: 128 (over y_hi, z, x).
Axes of the slice: x: 4, y: 4 (y_hi: 2, y_lo: 2; y = y_hi * 2 + y_lo), z: 16, core: 2. Of those that a mesh axis runs over, the one named last changes fastest.
Arguments:
- history: bfloat16 [128, 128, 1536], P('shard'), may hold values from -10 to 10
- lengths: int32 [128], P('shard'), may hold values from 1 to 128, 10240 in all
- beam_ids: int32 [128, 4, 32], P('shard', 'role'), may hold values from 0 to 255
- routes: int32 [128, 4, 32, 2], P('shard', 'role'), may hold values from 0 to 63, all different within a row; in each aligned block of 32 rows (0 to 31, 32 to 63, ..., all dimensions but the last counted through in order) at most 2 rows name the same one
- code_table: bfloat16 [1024, 1536], P('role'), may hold values from -8 to 8
- w_key: bfloat16 [1536, 1536], P('shard', 'role'), may hold values from -1 to 1
- w_value: bfloat16 [1536, 1536], P('shard', 'role'), may hold values from -0.15625 to 0.15625
- w_query: bfloat16 [1536, 1536], P('shard', 'role'), may hold values from -9 to 9
- w_out: bfloat16 [1536, 1536], P('role', 'shard'), may hold values from -0.15625 to 0.15625
- norm_gain: float32 [1536], replicated, may hold values from 0.5 to 1.5
- moe_gain: float32 [1536], replicated, may hold values from 0.5 to 1.5
- w_router: bfloat16 [1536, 64], replicated, may hold values from -0.15625 to 0.15625
- w_gate: bfloat16 [512, 1536, 384], P(('role', 'shard')), may hold values from -0.15625 to 0.15625
- w_up: bfloat16 [512, 1536, 384], P(('role', 'shard')), may hold values from -0.15625 to 0.15625
- w_down: bfloat16 [512, 384, 1536], P(('role', 'shard')), may hold values from -0.109375 to 0.109375
Outputs:
- layer_out: bfloat16 [128, 4, 32, 1536], P('shard', 'role')
The draws below stay inside these ranges and needn't reach their ends.
Inputs may be any that keep to these rules, and one draw needn't show every extreme that they name: `lengths`: at most 128, and some request has exactly 128. `routes`: each row names two different experts; among the 32 rows of one request and level no expert is named more than 2 times, a bound that some block reaches.
All inputs are finite; a program needn't handle non-finite values. No bound on the sum of `lengths` on one device may be relied on, other than what follows from the above.
Results may differ from the reference program's by a relative error of at most 0.015.
Values may be sent and summed in bfloat16 or wider, within the bound.
A program may use at most 64 MiB of HBM per device.

```python
import math
import jax
import jax.numpy as jnp
import numpy as np
from jax import lax

D = 1536
HEADS = 24
HID = 3072
SLICES = 8
LEVELS = 4
CODES = 256
HIST = 128
BEAMS = 32
REQS = 128
EXPERTS = 64
CAP = 2
DEVICES = 512


def draw_history(key, part):
    own_key = jax.random.fold_in(key, 11)
    return jnp.clip(jax.random.normal(own_key, (REQS, HIST, D), jnp.float32), -6.0, 6.0).astype(jnp.bfloat16)


def draw_code_table(key, part):
    own_key = jax.random.fold_in(key, 12)
    return jnp.clip(jax.random.normal(own_key, (LEVELS * CODES, D), jnp.float32), -6.0, 6.0).astype(jnp.bfloat16)


def draw_w_key(key, part):
    own_key = jax.random.fold_in(key, 13)
    return (jnp.clip(jax.random.normal(own_key, (D, D), jnp.float32), -6.0, 6.0) * D ** (-0.5)).astype(jnp.bfloat16)


def draw_w_query(key, part):
    own_key = jax.random.fold_in(key, 14)
    return (jnp.clip(jax.random.normal(own_key, (D, D), jnp.float32), -6.0, 6.0) * D ** (-0.5)).astype(jnp.bfloat16)


def set_ends(values, key, least, largest):
    dims = values.shape
    place = [jax.random.randint(jax.random.fold_in(key, axis), (), 0, dims[axis]) for axis in range(len(dims))]
    values = values.at[tuple(place)].set(least)
    longest = dims.index(max(dims))
    place[longest] = (place[longest] + 1) % dims[longest]
    return values.at[tuple(place)].set(largest)


def block_levels(stream_key, shape, cuts, least, high):
    def one(dim, parts):
        steps = jax.random.uniform(jax.random.fold_in(jax.random.fold_in(stream_key, 6), dim), (parts,), jnp.float32, least / len(cuts), high / len(cuts))
        return jnp.repeat(jnp.exp(steps), shape[dim] // parts).reshape((-1,) + (1,) * (len(shape) - dim - 1))

    factor_of = one(*cuts[0])
    for cut in cuts[1:]:
        factor_of = factor_of * one(*cut)
    return factor_of


def split_up(number_of, total, bound, lean):
    portions = [(1 << 20) // math.isqrt(grade ** lean) + 1 for grade in range(2, number_of + 1)]
    spare, holding = total - bound - (number_of - 1), [1] * (number_of - 1)
    while spare > 0:
        free = [i for i in range(number_of - 1) if holding[i] < bound]
        pool, budget = sum([portions[i] for i in free]), spare
        for i in free:
            more = min(bound - holding[i], max(1, budget * portions[i] // pool), spare)
            holding[i] = holding[i] + more
            spare = spare - more
    return np.array([bound] + holding)


def ragged(key, number_of, total, most, lean):
    if number_of == 2:
        one = jax.random.randint(key, (), max(1, total - most), min(most, total - 1) + 1)
        return jnp.stack([one, total - one])
    sizes = jnp.asarray(split_up(number_of, total, most, lean), jnp.int32)
    couples = (number_of - 1) // 2
    donor, taker = sizes[1:1 + 2 * couples:2], sizes[2:2 + 2 * couples:2]
    room = jnp.minimum(donor - 1, most - taker)
    shifted = jax.random.randint(jax.random.fold_in(key, 1), (couples,), 0, 1 << 20) % (room + 1)
    sizes = sizes.at[1:1 + 2 * couples:2].set(donor - shifted).at[2:2 + 2 * couples:2].set(taker + shifted)
    return sizes[jax.random.permutation(jax.random.fold_in(key, 2), number_of)]


def deal_out(key, own, number, rows, number_of, top, most, lean):
    sequence = jax.random.permutation(key, number_of)
    crowded, common = portions_of(number_of, rows * top, most, lean, True), portions_of(number_of, rows * top, most, lean, False)
    places = jnp.arange(number_of)

    def named(sizes, turn):
        used = int((sizes > 0).sum())
        fixed = max(1, used // 4)
        passed = fixed + (places - fixed + turn * (used - fixed)) % max(1, number_of - fixed)
        return jnp.zeros((number_of,), jnp.int32).at[sequence[jnp.where(places < fixed, places, passed)]].set(jnp.asarray(sizes, jnp.int32))

    sizes = jnp.where(number % 4 == 0, named(crowded, number // 4), named(common, number - number // 4 - 1))
    mixed = jax.random.permutation(jax.random.fold_in(own, 3), number_of)
    giver, taker = mixed[0:number_of // 2 * 2:2], mixed[1:number_of // 2 * 2:2]
    room = jnp.minimum(sizes[giver] - 1, most - sizes[taker]) // 2
    room = jnp.where((giver == sequence[0]) | (taker == sequence[0]) | (sizes[taker] == 0), 0, jnp.maximum(room, 0))
    passed = jax.random.randint(jax.random.fold_in(own, 4), (number_of // 2,), 0, 1 << 20) % (room + 1)
    sizes = sizes.at[giver].add(-passed).at[taker].add(passed)
    labels = jnp.searchsorted(jnp.cumsum(sizes), jnp.arange(rows * top), side="right").astype(jnp.int32)
    grid = labels.reshape(top, rows).T
    grid = grid[jax.random.permutation(jax.random.fold_in(own, 1), rows)]
    turn = jax.random.randint(jax.random.fold_in(own, 2), (rows, 1), 0, top)
    return jnp.take_along_axis(grid, (jnp.arange(top)[None, :] + turn) % top, axis=1)


def portions_of(count, total, limit, skew, full):
    weights = [(1 << 20) // math.isqrt(grade ** skew) + 1 for grade in range(1, count + 1)]
    largest = limit if full else min(limit, max(-(-total // count), total * weights[0] // sum(weights)))
    least = 1 if total - largest >= count - 1 else 0
    given, rest = [largest] + [least] * (count - 1), total - largest - least * (count - 1)
    while rest > 0:
        free = [i for i in range(1, count) if given[i] < largest] or [i for i in range(1, count) if given[i] < limit]
        pool, budget = sum([weights[i] for i in free]), rest
        for i in free:
            more = min(limit - given[i], max(1, budget * weights[i] // pool), rest)
            given[i] = given[i] + more
            rest = rest - more
    return np.array(given)


def centred(rng, shape, spread, reach, pieces=(), held_as=jnp.bfloat16):
    loudness = block_levels(rng, shape, pieces, -0.22, 0.18) if pieces else 1.0
    values = jax.random.normal(rng, shape, jnp.float32) * spread * loudness
    return jnp.minimum(jnp.maximum(values, -reach), reach).astype(held_as)


def setup_inputs(seed: int = 0) -> dict:
    arg_keys = jax.random.split(jax.random.key(seed), 16)
    history = draw_history(jax.random.fold_in(arg_keys[15], 71), 0)
    lengths = ragged(arg_keys[1], REQS, REQS * HIST * 5 // 8, HIST, 1).astype(jnp.int32)
    beam_ids = set_ends(jax.random.randint(arg_keys[2], (REQS, LEVELS, BEAMS), 0, CODES), jax.random.fold_in(arg_keys[2], 1), 0, CODES - 1).astype(jnp.int32)
    routes_keys = jax.random.split(jax.random.fold_in(arg_keys[3], 1), REQS * LEVELS * BEAMS // BEAMS)
    routes_turns = jax.random.permutation(jax.random.fold_in(arg_keys[3], 3), REQS * LEVELS * BEAMS // BEAMS)
    routes = jax.vmap(lambda own, number: deal_out(jax.random.fold_in(arg_keys[3], 2), own, number, BEAMS, EXPERTS, 2, CAP, 2))(routes_keys, routes_turns).reshape((REQS, LEVELS, BEAMS, 2))
    code_table = draw_code_table(jax.random.fold_in(arg_keys[15], 71), 0)
    w_key = draw_w_key(jax.random.fold_in(arg_keys[15], 71), 0)
    w_value = centred(arg_keys[6], (D, D), D ** -0.5, 0.15625, ((0, 128), (1, 4)))
    w_query = draw_w_query(jax.random.fold_in(arg_keys[15], 71), 0)
    w_out = centred(arg_keys[8], (D, D), D ** -0.5, 0.15625, ((0, 4), (1, 128)))
    norm_gain = jnp.clip(1.0 + 0.1 * jax.random.normal(arg_keys[9], (D,), jnp.float32), 0.5, 1.5)
    moe_gain = jnp.clip(1.0 + 0.1 * jax.random.normal(arg_keys[10], (D,), jnp.float32), 0.5, 1.5)
    w_router = centred(arg_keys[11], (D, EXPERTS), D ** -0.5, 0.15625)
    w_gate = centred(arg_keys[12], (DEVICES, D, HID // SLICES), D ** -0.5, 0.15625, ((0, 512),))
    w_up = centred(arg_keys[13], (DEVICES, D, HID // SLICES), D ** -0.5, 0.15625, ((0, 512),))
    w_down = centred(arg_keys[14], (DEVICES, HID // SLICES, D), HID ** -0.5, 0.109375, ((0, 512),))
    return dict(history=history, lengths=lengths, beam_ids=beam_ids, routes=routes, code_table=code_table, w_key=w_key, w_value=w_value, w_query=w_query, w_out=w_out, norm_gain=norm_gain, moe_gain=moe_gain, w_router=w_router, w_gate=w_gate, w_up=w_up, w_down=w_down)


eps = 1e-06

def norm_rows(values, scale_vec):
    values = values.astype(jnp.float32)
    power = lax.optimization_barrier(jnp.mean(values * values, axis=-1, keepdims=True))
    return values * lax.rsqrt(power + eps) * scale_vec.astype(jnp.float32)

def reference(history, lengths, beam_ids, routes, code_table, w_key, w_value, w_query, w_out, norm_gain, moe_gain, w_router, w_gate, w_up, w_down):
    head_dim = D // HEADS
    table_index = (jnp.arange(LEVELS, dtype=jnp.int32)[None, :, None] * CODES + beam_ids).astype(jnp.int32)
    embedded = code_table[table_index]
    normed = norm_rows(embedded, norm_gain).astype(jnp.bfloat16)

    def attend(packed):
        events, count, query_rows = packed
        keys = jnp.dot(events, w_key, preferred_element_type=jnp.float32).astype(jnp.bfloat16)
        values = jnp.dot(events, w_value, preferred_element_type=jnp.float32).astype(jnp.bfloat16)
        queries = jnp.dot(query_rows, w_query, preferred_element_type=jnp.float32).astype(jnp.bfloat16)
        query_heads = queries.reshape(-1, HEADS, head_dim).astype(jnp.float32)
        key_heads = keys.reshape(-1, HEADS, head_dim).astype(jnp.float32)
        value_heads = values.reshape(-1, HEADS, head_dim).astype(jnp.float32)
        scores = jnp.einsum('rhd,jhd->hrj', query_heads, key_heads) * head_dim ** (-0.5)
        visible = jnp.arange(events.shape[0], dtype=jnp.int32) < count
        scores = jnp.where(visible[None, None, :], scores, -1e+30)
        top_score = lax.optimization_barrier(jnp.max(scores, axis=-1, keepdims=True))
        weights = jnp.exp(scores - top_score)
        probs = (weights / lax.optimization_barrier(jnp.sum(weights, axis=-1, keepdims=True))).astype(jnp.bfloat16)
        mixed = jnp.einsum('hrj,jhd->rhd', probs.astype(jnp.float32), value_heads).astype(jnp.bfloat16)
        return jnp.dot(mixed.reshape(-1, D), w_out, preferred_element_type=jnp.float32)
    attended = lax.map(attend, (history, lengths, normed.reshape(REQS, LEVELS * BEAMS, D)))
    hidden = (embedded.astype(jnp.float32).reshape(REQS, LEVELS * BEAMS, D) + attended).astype(jnp.bfloat16)
    flat_hidden = hidden.reshape(-1, D)
    moe_in = norm_rows(flat_hidden, moe_gain).astype(jnp.bfloat16)
    logits = jnp.dot(moe_in, w_router, preferred_element_type=jnp.float32)
    pairs = routes.reshape(-1, 2)
    picked = jnp.take_along_axis(logits, pairs, axis=1)
    gates = jax.nn.softmax(picked, axis=-1)
    block_count = REQS * LEVELS
    per_block = pairs.reshape(block_count, BEAMS * 2)
    member = (per_block[..., None] == jnp.arange(EXPERTS, dtype=jnp.int32)).astype(jnp.int32)
    before = jnp.cumsum(member, axis=1) - member
    slot_index = lax.optimization_barrier(jnp.sum(before * member, axis=-1))
    position = (jnp.arange(block_count, dtype=jnp.int32)[:, None] * CAP + slot_index).astype(jnp.int32)
    doubled = jnp.repeat(moe_in, 2, axis=0)
    buffers = jnp.zeros((EXPERTS, block_count * CAP, D), jnp.bfloat16)
    buffers = buffers.at[per_block.reshape(-1), position.reshape(-1)].set(doubled)
    gate_parts = w_gate.reshape(EXPERTS, SLICES, D, HID // SLICES)
    up_parts = w_up.reshape(EXPERTS, SLICES, D, HID // SLICES)
    down_parts = w_down.reshape(EXPERTS, SLICES, HID // SLICES, D)

    def expert(packed):
        rows_in, gate_w, up_w, down_w = packed
        total = jnp.zeros((rows_in.shape[0], D), jnp.float32)
        for portion in range(SLICES):
            gate_val = jnp.dot(rows_in, gate_w[portion], preferred_element_type=jnp.float32)
            up_val = jnp.dot(rows_in, up_w[portion], preferred_element_type=jnp.float32)
            inner = (jax.nn.silu(gate_val) * up_val).astype(jnp.bfloat16)
            rounded = jnp.dot(inner, down_w[portion], preferred_element_type=jnp.float32).astype(jnp.bfloat16)
            rounded = lax.optimization_barrier(rounded)
            total = total + rounded.astype(jnp.float32)
        return total.astype(jnp.bfloat16)
    expert_out = lax.map(expert, (buffers, gate_parts, up_parts, down_parts))
    fetched = expert_out[per_block.reshape(-1), position.reshape(-1)].reshape(-1, 2, D).astype(jnp.float32)
    result = flat_hidden.astype(jnp.float32) + lax.optimization_barrier(jnp.sum(gates[..., None] * fetched, axis=1))
    return result.astype(jnp.bfloat16).reshape(REQS, LEVELS, BEAMS, D)
```

```python
import functools

import jax
import jax.numpy as jnp
from jax import lax
from jax.experimental import pallas as pl
from jax.experimental.pallas import tpu as pltpu
from jax.sharding import PartitionSpec as P

MESH = pl.DeviceIdType.MESH
F32, BF16, I32 = jnp.float32, jnp.bfloat16, jnp.int32
D = 1536
HEAD = 64
OWN = 384
ROWS = 32
EPS = 1e-06


class Here:
    def __init__(self):
        role, shard = lax.axis_index("role"), lax.axis_index("shard")
        self.role = role
        self.y_lo, self.core = role // 2, role % 2
        self.y_hi, self.z, self.x = shard // 64, (shard // 4) % 16, shard % 4
        self.y = self.y_hi * 2 + self.y_lo

    def to(self, y_hi=None, y_lo=None, core=None, z=None, x=None):
        pick = lambda new, old: old if new is None else new
        y_hi, y_lo, core = pick(y_hi, self.y_hi), pick(y_lo, self.y_lo), pick(core, self.core)
        z, x = pick(z, self.z), pick(x, self.x)
        return (y_lo * 2 + core, y_hi * 64 + z * 4 + x)


def put(src, dst, send, recv, to):
    pltpu.make_async_remote_copy(
        src_ref=src, dst_ref=dst, send_sem=send, recv_sem=recv, device_id=to, device_id_type=MESH
    ).start()


def put_or_keep(is_self, src, dst, send, recv, to):
    @pl.when(is_self)
    def _():
        pltpu.make_async_copy(src, dst, recv).start()

    @pl.when(jnp.logical_not(is_self))
    def _():
        put(src, dst, send, recv, to)


def done(ref, sem):
    pltpu.make_async_copy(ref, ref, sem).wait()


def done_unless(is_self, ref, sem):
    @pl.when(jnp.logical_not(is_self))
    def _():
        done(ref, sem)


def greet(targets):
    barrier = pltpu.get_barrier_semaphore()
    for to in targets:
        pl.semaphore_signal(barrier, inc=1, device_id=to, device_id_type=MESH)
    pl.semaphore_wait(barrier, len(targets))


def norm_rows(values, gain):
    power = jnp.mean(values * values, axis=-1, keepdims=True)
    return (values * lax.rsqrt(power + EPS) * gain).astype(BF16)


def mm(a, b):
    return jnp.dot(a, b, preferred_element_type=F32)


def mm_nt(a, b):
    return lax.dot_general(a, b, (((1,), (1,)), ((), ())), preferred_element_type=F32)


def iota(shape, dim):
    return lax.broadcasted_iota(I32, shape, dim)


def attend_kernel(
    ids, lens, gain, piece, table, hist,
    hidden,
    emb, every, events, len_out, len_in, by_x, w, part, parts,
    x_send, x_recv, e_send, e_recv, h_send, h_recv, f_send, f_recv, b_send, b_recv,
    c_send, c_recv, r_send, r_recv,
):
    me = Here()
    straight = me.y_hi == me.core
    column = []
    for k in range(8):
        if k:
            d = (me.y * 2 + me.core + k) % 8
            column.append(me.to(y_hi=d // 4, y_lo=(d // 2) % 2, core=d % 2))
    rows_x = [me.to(y_hi=me.core, core=me.y_hi, x=(me.x + k) % 4) for k in range(4)]
    up, down = me.to(z=(me.z + 1) % 16), me.to(z=(me.z + 15) % 16)
    other = me.to(core=1 - me.core)
    greet(column + rows_x[1:] + [up, down])

    for k in range(4):
        args = (piece, by_x.at[me.x], x_send.at[k], x_recv.at[me.x], rows_x[k])
        if k:
            put(*args)
        else:
            put_or_keep(straight, *args)

    len_out[...] = jnp.full((8, 128), lens[0], I32)
    put_or_keep(straight, hist, events, h_send.at[0], h_recv.at[0], rows_x[0])
    put_or_keep(straight, len_out, len_in, h_send.at[1], h_recv.at[1], rows_x[0])

    lookup = (ids[...] == iota((ROWS, table.shape[0]), 1)).astype(BF16)
    emb[...] = mm(lookup, table[...]).astype(BF16)
    for k in range(4):
        y = (me.y + k) % 4
        args = (emb, every.at[me.role], e_send.at[k], e_recv.at[me.role],
                me.to(y_hi=y // 2, y_lo=y % 2, core=me.y_hi))
        if k:
            put(*args)
        else:
            put_or_keep(straight, *args)

    for k in range(4):
        done(by_x.at[k], x_recv.at[k])
    o, i = iota((192, 192), 0), iota((192, 192), 1)
    source = ((o % 48) // 12) * 48 + (o // 48) * 12 + o % 12
    ordered = mm((source == i).astype(BF16), by_x[...].reshape(192, OWN)).astype(BF16)

    def block(z, c):
        return w.at[pl.ds(2 * c, 2), pl.ds(pl.multiple_of(me.core * 768 + z * 48, 16), 48), :]

    for c in range(2):
        block(me.z, c)[...] = ordered[96 * c : 96 * c + 96].reshape(2, 48, OWN)

    for c in range(2):
        put(block(me.z, c), block(me.z, c), f_send.at[0, c], f_recv.at[0, c], up)
        put(block(me.z, c), block(me.z, c), b_send.at[0, c], b_recv.at[0, c], down)
        put(block(me.z, c), block(me.z, c), c_send, c_recv, other)
    for t in range(1, 9):
        fz, bz = (me.z + 16 - t) % 16, (me.z + t) % 16
        for c in range(2):
            for z, send, recv, to, last in ((fz, f_send, f_recv, up, 0), (bz, b_send, b_recv, down, 1)):
                if t == 8 and c != last:
                    continue
                done(block(z, c), recv.at[t - 1, c])
                if t < 7 or (t == 7 and c == last):
                    put(block(z, c), block(z, c), send.at[t, c], recv.at[t, c], to)
                put(block(z, c), block(z, c), c_send, c_recv, other)

    for k in range(4):
        done(every.at[k], e_recv.at[k])
    normed = norm_rows(every[...].reshape(4 * ROWS, D).astype(F32), gain[...])
    done(events, h_recv.at[0])
    done(len_in, h_recv.at[1])
    half = w.at[:, pl.ds(pl.multiple_of((1 - me.core) * 768, 16), 768), :]
    done(half, c_recv)

    keys = mm(events[...], w[0]).astype(BF16)
    values = mm(events[...], w[1]).astype(BF16)
    queries = mm(normed, w[2]).astype(BF16)
    visible = iota((128, 128), 1) < len_in[0:1, :]
    low = iota((128, 128), 1) < HEAD
    mixed = []
    for pair in range(OWN // 128):
        cut = slice(128 * pair, 128 * pair + 128)
        q, k, v = queries[:, cut], keys[:, cut], values[:, cut]
        outs = []
        for mask in (low, jnp.logical_not(low)):
            scores = mm_nt(jnp.where(mask, q, jnp.zeros_like(q)), k) * HEAD ** -0.5
            scores = jnp.where(visible, scores, -1e30)
            weights = jnp.exp(scores - jnp.max(scores, axis=-1, keepdims=True))
            probs = (weights / jnp.sum(weights, axis=-1, keepdims=True)).astype(BF16)
            outs.append(mm(probs, v))
        mixed.append(jnp.where(low, outs[0], outs[1]).astype(BF16))
    mixed = jnp.concatenate(mixed, axis=1)
    part[...] = mm_nt(mixed, w[3]).astype(BF16).reshape(4, ROWS, D)

    for level in range(4):
        own = jnp.logical_and(straight, me.role == level)
        put_or_keep(own, part.at[level], parts.at[me.y], r_send.at[level], r_recv.at[me.y],
                    me.to(y_hi=me.core, y_lo=level // 2, core=level % 2))
    total = jnp.zeros((ROWS, D), F32)
    for k in range(4):
        done(parts.at[k], r_recv.at[k])
    for k in range(4):
        total += parts[k].astype(F32)
    hidden[...] = (emb[...].astype(F32) + total).astype(BF16)

    for k in range(4):
        if k:
            done(piece, x_send.at[k])
            done(emb, e_send.at[k])
        else:
            done_unless(straight, piece, x_send.at[k])
            done_unless(straight, emb, e_send.at[k])
        own = jnp.logical_and(straight, me.role == k)
        done_unless(own, part.at[k], r_send.at[k])
    done_unless(straight, events, h_send.at[0])
    done_unless(straight, len_out, h_send.at[1])
    for t in range(8):
        for c in range(2):
            if t < 7 or c == 0:
                done(block(me.z, c), f_send.at[t, c])
            if t < 7 or c == 1:
                done(block(me.z, c), b_send.at[t, c])
    done(half, c_send)


def expert_kernel(
    hid, routes, routes_t, gain, router, wg_hbm, wu_hbm, wd_hbm,
    out,
    wg, wu, wd, packed, got_y, sorted_z, rows, res, sums, z_out, z_in, done_rows, back_z, sorted_y, back_y,
    w_sem, y_send, y_recv, z_send, z_recv, p_send, p_recv, x_send, x_recv, s_send, s_recv,
    q_send, q_recv, bz_send, bz_recv, by_send, by_recv,
):
    me = Here()
    col = me.y_lo * 4 + me.core * 2 + me.y_hi
    zp, z_lo = me.z // 2, me.z % 2

    def in_column(d):
        return me.to(y_lo=d // 4, core=(d // 2) % 2, y_hi=d % 2)

    def in_z(p):
        return me.to(z=p * 2 + z_lo)

    mate = me.to(z=zp * 2 + 1 - z_lo)
    x_of = [(me.x + k) % 4 for k in range(4)]
    greet([in_column((col + k) % 8) for k in range(1, 8)]
          + [in_z((zp + k) % 8) for k in range(1, 8)]
          + [mate] + [me.to(x=x_of[k]) for k in range(1, 4)])

    for k, (src, dst) in enumerate(((wg_hbm, wg), (wu_hbm, wu), (wd_hbm, wd))):
        pltpu.make_async_copy(src, dst, w_sem.at[k]).start()

    hidden = hid[...].astype(F32)
    moe_in = norm_rows(hidden, gain[...])

    def slots(shape, dim):
        slot = iota(shape, dim)
        return (slot // 16) * 8 + slot % 8, (slot // 8) % 2

    expert, order = slots((128, ROWS), 0)
    named = jnp.logical_or(routes_t[0:1, :] == expert, routes_t[1:2, :] == expert)
    earlier = (iota((ROWS, ROWS), 0) < iota((ROWS, ROWS), 1)).astype(BF16)
    before = mm(named.astype(BF16), earlier)
    placing = jnp.logical_and(named, before == order.astype(F32)).astype(BF16)
    packed[...] = mm(placing, moe_in).astype(BF16)

    def cut(ref, k):
        return ref.at[pl.ds(pl.multiple_of(k * 16, 16), 16), :]

    pltpu.make_async_copy(cut(packed, col), cut(got_y, col), y_recv.at[col]).start()
    for k in range(1, 8):
        d = (col + k) % 8
        put(cut(packed, d), cut(got_y, col), y_send.at[k], y_recv.at[col], in_column(d))
    for k in range(8):
        done(cut(got_y, k), y_recv.at[k])
    o, i = iota((128, 128), 0), iota((128, 128), 1)
    source = ((o // 2) % 8) * 16 + (o % 2) * 8 + o // 16
    sorted_z[...] = mm((source == i).astype(BF16), got_y[...]).astype(BF16)

    mine = rows.at[me.x, z_lo]
    pltpu.make_async_copy(cut(sorted_z, zp), cut(mine, zp), z_recv.at[zp]).start()
    for k in (4, 3, 5, 2, 6, 1, 7):
        p = (zp + k) % 8
        put(cut(sorted_z, p), cut(mine, zp), z_send.at[k], z_recv.at[zp], in_z(p))

    logits = mm(moe_in, router[...])
    lanes = iota(logits.shape, 1)
    picked = [
        jnp.sum(jnp.where(routes[:, k : k + 1] == lanes, logits, 0.0), axis=-1, keepdims=True)
        for k in range(2)
    ]
    top = jnp.maximum(picked[0], picked[1])
    powers = [jnp.exp(p - top) for p in picked]
    gates = [p / (powers[0] + powers[1]) for p in powers]
    expert_l, order_l = slots((ROWS, 128), 1)
    member = [routes[:, k : k + 1] == expert_l for k in range(2)]
    later = (iota((ROWS, ROWS), 1) < iota((ROWS, ROWS), 0)).astype(BF16)
    before_l = mm(later, jnp.logical_or(member[0], member[1]).astype(BF16))
    taking = [jnp.logical_and(m, before_l == order_l.astype(F32)).astype(BF16) for m in member]

    for k in range(8):
        done(cut(mine, k), z_recv.at[k])
    put(mine, mine, p_send, p_recv, mate)
    done(rows.at[me.x, 1 - z_lo], p_recv)
    for k in (2, 1, 3):
        put(rows.at[me.x], rows.at[me.x], x_send.at[k], x_recv.at[me.x], me.to(x=x_of[k]))

    for k, dst in enumerate((wg, wu, wd)):
        done(dst, w_sem.at[k])

    def apply(x):
        here = rows[x].reshape(256, D)
        gate, up = mm(here, wg[...]), mm(here, wu[...])
        inner = (gate / (1.0 + jnp.exp(-gate)) * up).astype(BF16)
        res[x] = mm(inner, wd[...]).astype(BF16).reshape(2, 128, D)

    apply(me.x)
    for k in (1, 3, 2):
        x = x_of[k]
        done(rows.at[x], x_recv.at[x])
        apply(x)
        put(res.at[x], sums.at[me.x], s_send.at[k], s_recv.at[me.x], me.to(x=x))
    for k in range(1, 4):
        done(sums.at[x_of[k]], s_recv.at[x_of[k]])

    def total(z):
        value = res[me.x, z].astype(F32)
        for k in range(1, 4):
            value += sums[x_of[k], z].astype(F32)
        return value

    z_out[...] = total(1 - z_lo).astype(BF16)
    put(z_out, z_in, q_send, q_recv, mate)
    own = total(z_lo)
    done(z_in, q_recv)
    done_rows[...] = (own + z_in[...].astype(F32)).astype(BF16)

    pltpu.make_async_copy(cut(done_rows, zp), cut(back_z, zp), bz_recv.at[zp]).start()
    for k in (4, 3, 5, 2, 6, 1, 7):
        p = (zp + k) % 8
        put(cut(done_rows, p), cut(back_z, zp), bz_send.at[k], bz_recv.at[zp], in_z(p))
    for k in range(8):
        done(cut(back_z, k), bz_recv.at[k])
    source = (o % 8) * 16 + (o // 16) * 2 + (o // 8) % 2
    sorted_y[...] = mm((source == i).astype(BF16), back_z[...]).astype(BF16)
    pltpu.make_async_copy(cut(sorted_y, col), cut(back_y, col), by_recv.at[col]).start()
    for k in range(1, 8):
        d = (col + k) % 8
        put(cut(sorted_y, d), cut(back_y, col), by_send.at[k], by_recv.at[col], in_column(d))
    for k in range(8):
        done(cut(back_y, k), by_recv.at[k])

    mixed = gates[0] * mm(taking[0], back_y[...]) + gates[1] * mm(taking[1], back_y[...])
    out[...] = (hidden + mixed).astype(BF16)

    for k in range(1, 8):
        for ref, sem in ((packed, y_send), (sorted_z, z_send), (done_rows, bz_send), (sorted_y, by_send)):
            done(cut(ref, 0), sem.at[k])
    done(mine, p_send)
    for k in range(1, 4):
        done(rows.at[me.x], x_send.at[k])
        done(res.at[me.x], s_send.at[k])
    done(z_out, q_send)


def dma(*shape):
    return pltpu.SemaphoreType.DMA(shape)


def vmem(*shape, dtype=BF16):
    return pltpu.VMEM(shape, dtype)


VM = pl.BlockSpec(memory_space=pltpu.VMEM)
SM = pl.BlockSpec(memory_space=pltpu.SMEM)
ANY = pl.BlockSpec(memory_space=pl.ANY)


def shards(history, lengths, beam_ids, routes, code_table, w_key, w_value, w_query, w_out,
           norm_gain, moe_gain, w_router, w_gate, w_up, w_down):
    piece = jnp.concatenate([w_key, w_value, w_query, w_out.T], axis=0)
    hidden = pl.pallas_call(
        attend_kernel,
        out_shape=jax.ShapeDtypeStruct((ROWS, D), BF16),
        in_specs=[VM, SM, VM, VM, VM, ANY],
        out_specs=VM,
        scratch_shapes=[
            vmem(ROWS, D), vmem(4, ROWS, D), vmem(128, D), vmem(8, 128, dtype=I32), vmem(8, 128, dtype=I32),
            vmem(4, 48, OWN), vmem(4, D, OWN), vmem(4, ROWS, D), vmem(4, ROWS, D),
            dma(4), dma(4), dma(4), dma(4), dma(2), dma(2), dma(8, 2), dma(8, 2), dma(8, 2), dma(8, 2),
            pltpu.SemaphoreType.DMA, pltpu.SemaphoreType.DMA, dma(4), dma(4),
        ],
        compiler_params=pltpu.CompilerParams(
            collective_id=0, has_side_effects=True, vmem_limit_bytes=48 * 1024 * 1024
        ),
        name="attend",
    )(beam_ids.reshape(ROWS, 1), lengths, norm_gain.reshape(1, D), piece, code_table, history.reshape(128, D))
    pairs = routes.reshape(ROWS, 2)
    result = pl.pallas_call(
        expert_kernel,
        out_shape=jax.ShapeDtypeStruct((ROWS, D), BF16),
        in_specs=[VM] * 5 + [ANY] * 3,
        out_specs=VM,
        scratch_shapes=[
            vmem(D, OWN), vmem(D, OWN), vmem(OWN, D), vmem(128, D), vmem(128, D), vmem(128, D),
            vmem(4, 2, 128, D), vmem(4, 2, 128, D), vmem(4, 2, 128, D), vmem(128, D), vmem(128, D),
            vmem(128, D), vmem(128, D), vmem(128, D), vmem(128, D),
            dma(3), dma(8), dma(8), dma(8), dma(8),
            pltpu.SemaphoreType.DMA, pltpu.SemaphoreType.DMA, dma(4), dma(4), dma(4), dma(4),
            pltpu.SemaphoreType.DMA, pltpu.SemaphoreType.DMA, dma(8), dma(8), dma(8), dma(8),
        ],
        compiler_params=pltpu.CompilerParams(
            collective_id=1, has_side_effects=True, vmem_limit_bytes=48 * 1024 * 1024
        ),
        name="experts",
    )(hidden, pairs, pairs.T, moe_gain.reshape(1, D), w_router, w_gate[0], w_up[0], w_down[0])
    return result.reshape(1, 1, ROWS, D)


def solution(mesh):
    return jax.shard_map(
        shards,
        mesh=mesh,
        in_specs=(
            P("shard", None, None),
            P("shard"),
            P("shard", "role", None),
            P("shard", "role", None, None),
            P("role", None),
            P("shard", "role"),
            P("shard", "role"),
            P("shard", "role"),
            P("role", "shard"),
            P(),
            P(),
            P(),
            P(("role", "shard"), None, None),
            P(("role", "shard"), None, None),
            P(("role", "shard"), None, None),
        ),
        out_specs=P("shard", "role", None, None),
        check_vma=False,
    )
```

```python
import functools

import jax
import jax.numpy as jnp
from jax import lax
from jax.experimental import pallas as pl
from jax.experimental.pallas import tpu as pltpu
from jax.sharding import PartitionSpec as P

MESH = pl.DeviceIdType.MESH
F32, BF16, I32 = jnp.float32, jnp.bfloat16, jnp.int32
D = 1536
HEAD = 64
OWN = 384
ROWS = 32
EPS = 1e-06


class Here:
    def __init__(self):
        role, shard = lax.axis_index("role"), lax.axis_index("shard")
        self.role = role
        self.y_lo, self.core = role // 2, role % 2
        self.y_hi, self.z, self.x = shard // 64, (shard // 4) % 16, shard % 4
        self.y = self.y_hi * 2 + self.y_lo

    def to(self, y_hi=None, y_lo=None, core=None, z=None, x=None):
        pick = lambda new, old: old if new is None else new
        y_hi, y_lo, core = pick(y_hi, self.y_hi), pick(y_lo, self.y_lo), pick(core, self.core)
        z, x = pick(z, self.z), pick(x, self.x)
        return (y_lo * 2 + core, y_hi * 64 + z * 4 + x)


def done(ref, sem):
    pltpu.make_async_copy(ref, ref, sem).wait()


def norm_rows(values, gain):
    power = jnp.mean(values * values, axis=-1, keepdims=True)
    return (values * lax.rsqrt(power + EPS) * gain).astype(BF16)


def mm(a, b):
    return jnp.dot(a, b, preferred_element_type=F32)


def mm_nt(a, b):
    return lax.dot_general(a, b, (((1,), (1,)), ((), ())), preferred_element_type=F32)


def iota(shape, dim):
    return lax.broadcasted_iota(I32, shape, dim)


ORDER = (1, 2, 3, 0)
CHUNKS = len(ORDER)
LEAD = 2
LAG = (2, 4)
FORWARD = (1, 2)
BACKWARD = (1, 2, 3)


def layer_kernel(
    ids, lens, routes_t, gain, moe_gain, w_key, w_value, w_query, w_out_t, router_t, table_hbm, hist,
    wg_hbm, wu_hbm, wd_hbm,
    out,
    table, emb, every, events, len_out, len_in, piece, raw, w, part, parts,
    wg, wu, wd, packed, got_y, sorted_z, rows, res, halves, sums, z_out, z_in, fin, back_z, sorted_y, back_y,
    t_sem, w_sem, m_send, m_recv, e_send, e_recv, hi_send, hi_recv, f_send, f_recv, b_send, b_recv,
    d_send, d_recv, l_send, l_recv, c_send, c_recv, o_send, o_recv,
    y_send, y_recv, z_send, z_recv, p_send, p_recv, g_send, g_recv, r_send, r_recv,
    h_send, h_recv, s_send, s_recv, q_send, q_recv, bz_send, bz_recv, by_send, by_recv,
):
    me = Here()
    sent = []

    def put(src, dst, send, recv, to, listed=True):
        pltpu.make_async_remote_copy(
            src_ref=src, dst_ref=dst, send_sem=send, recv_sem=recv, device_id=to, device_id_type=MESH
        ).start()
        if listed:
            sent.append((src, send, None))

    def put_or_keep(is_self, src, dst, send, recv, to):
        @pl.when(is_self)
        def _():
            pltpu.make_async_copy(src, dst, recv).start()

        @pl.when(jnp.logical_not(is_self))
        def _():
            put(src, dst, send, recv, to, listed=False)

        sent.append((src, send, is_self))

    def all_left():
        for src, send, is_self in sent:
            if is_self is None:
                done(src, send)
            else:
                pl.when(jnp.logical_not(is_self))(functools.partial(done, src, send))

    straight = me.y_hi == me.core
    zp, z_lo = me.z // 2, me.z % 2
    col = me.y_lo * 4 + me.core * 2 + me.y_hi

    def in_column(d):
        return me.to(y_lo=d // 4, core=(d // 2) % 2, y_hi=d % 2)

    mirrored = [me.to(y_hi=me.core, core=me.y_hi, x=(me.x + k) % 4) for k in range(4)]
    other = me.to(core=1 - me.core)
    z_up, z_down = me.to(z=(me.z + 1) % 16), me.to(z=(me.z + 15) % 16)
    mate = me.to(z=zp * 2 + 1 - z_lo)
    x_up, x_far, x_down = [(me.x + k) % 4 for k in (1, 2, 3)]
    up, down = me.to(x=x_up), me.to(x=x_down)
    partners = ([in_column((col + k) % 8) for k in range(1, 8)] + mirrored[1:] + [z_up, z_down]
                + [me.to(z=(me.z + k) % 16) for k in range(2, 15)] + [up, down])
    barrier = pltpu.get_barrier_semaphore()
    for to in partners:
        pl.semaphore_signal(barrier, inc=1, device_id=to, device_id_type=MESH)

    pltpu.make_async_copy(table_hbm, table, t_sem).start()
    for k, (src, dst) in enumerate(((wg_hbm, wg), (wu_hbm, wu), (wd_hbm, wd))):
        pltpu.make_async_copy(src, dst, w_sem.at[k]).start()

    o, i = iota((48, 12), 0), iota((48, 12), 1)
    stacked = jnp.zeros((48, OWN), F32)
    for m, ref in enumerate((w_key, w_value, w_query, w_out_t)):
        stacked += mm((o == i + 12 * m).astype(BF16), ref[...])
    piece[...] = stacked.astype(BF16)
    len_out[...] = jnp.full((8, 128), lens[0], I32)
    eye = (iota((ROWS, ROWS), 0) == iota((ROWS, ROWS), 1)).astype(BF16)
    lookup = mm_nt(eye, (iota((256, ROWS), 0) == ids[...]).astype(BF16)).astype(BF16)
    done(table, t_sem)
    emb[...] = mm(lookup, table[...]).astype(BF16)

    pl.semaphore_wait(barrier, len(partners))

    put_or_keep(straight, piece, raw.at[me.x, me.z], m_send, m_recv, mirrored[0])

    o, i = iota((192, 192), 0), iota((192, 192), 1)
    ordering = (((o % 48) // 12) * 48 + (o // 48) * 12 + o % 12 == i).astype(BF16)

    def block(z):
        return w.at[:, pl.ds(pl.multiple_of(me.core * 768 + z * 48, 16), 48), :]

    def z_of(n):
        return (me.z + 16 - n) % 16 if n < 8 else (me.z + n - 7) % 16

    def share(n):
        mine = raw.at[me.x, z_of(n)]
        put(mine, mine, d_send.at[n, 0], d_recv.at[n, 0], up)
        put(mine, mine, d_send.at[n, 1], d_recv.at[n, 1], down)

    def pass_on(n):
        z = z_of(n)
        low, high = raw.at[x_down, z], raw.at[x_up, z]
        done(low, d_recv.at[n, 0])
        if n < 8:
            put(low, low, l_send.at[n], l_recv.at[n], up)
        done(high, d_recv.at[n, 1])
        if n >= 8:
            put(high, high, l_send.at[n], l_recv.at[n], down)

    def settle(n):
        z = z_of(n)
        done(raw.at[x_far, z], l_recv.at[n])
        pieces = jnp.concatenate([raw[x, z] for x in range(4)], axis=0)
        block(z)[...] = mm(ordering, pieces).astype(BF16).reshape(4, 48, OWN)
        put(block(z), block(z), c_send.at[n], c_recv, other)

    own_piece = raw.at[me.x, me.z]
    done(own_piece, m_recv)
    put(own_piece, own_piece, f_send.at[0], f_recv.at[0], z_up)
    put(own_piece, own_piece, b_send.at[0], b_recv.at[0], z_down)
    share(0)

    for k in range(4):
        y = (me.y + k) % 4
        args = (emb, every.at[me.role], e_send.at[k], e_recv.at[me.role],
                me.to(y_hi=y // 2, y_lo=y % 2, core=me.y_hi))
        if k:
            put(*args)
        else:
            put_or_keep(straight, *args)

    put_or_keep(straight, hist, events, hi_send.at[0], hi_recv.at[0], mirrored[0])
    put_or_keep(straight, len_out, len_in, hi_send.at[1], hi_recv.at[1], mirrored[0])

    def slots(shape, dim):
        slot = iota(shape, dim)
        return (slot // 16) * 8 + slot % 8, (slot // 8) % 2

    routes = mm_nt(eye, routes_t[...].astype(BF16)).astype(I32)
    expert, order = slots((128, ROWS), 0)
    named = jnp.logical_or(routes_t[0:1, :] == expert, routes_t[1:2, :] == expert)
    earlier = (iota((ROWS, ROWS), 0) < iota((ROWS, ROWS), 1)).astype(BF16)
    before = mm(named.astype(BF16), earlier)
    placing = jnp.logical_and(named, before == order.astype(F32)).astype(BF16)
    expert_l, order_l = slots((ROWS, 128), 1)
    member = [routes[:, k : k + 1] == expert_l for k in range(2)]
    later = (iota((ROWS, ROWS), 1) < iota((ROWS, ROWS), 0)).astype(BF16)
    before_l = mm(later, jnp.logical_or(member[0], member[1]).astype(BF16))
    taking = [jnp.logical_and(m, before_l == order_l.astype(F32)).astype(BF16) for m in member]

    def lagging(stage, t):
        if t == 0:
            stage(0)
        elif 0 < t < 8:
            stage(t)
            stage(t + 7)
        elif t == 8:
            stage(15)

    for t in range(1, 9 + LAG[1]):
        if t < 9:
            for n, send, recv, to in ((t, f_send, f_recv, z_up), (t + 7, b_send, b_recv, z_down)):
                if t == 8 and n == 8:
                    continue
                ref = raw.at[me.x, z_of(n)]
                done(ref, recv.at[t - 1])
                if t < 7 or (t == 7 and n == 14):
                    put(ref, ref, send.at[t], recv.at[t], to)
                share(n)
        lagging(pass_on, t - LAG[0])
        lagging(settle, t - LAG[1])

    for k in range(4):
        done(every.at[k], e_recv.at[k])
    normed = norm_rows(every[...].reshape(4 * ROWS, D).astype(F32), gain[...].reshape(1, D))
    done(events, hi_recv.at[0])
    done(len_in, hi_recv.at[1])
    half = w.at[:, pl.ds(pl.multiple_of((1 - me.core) * 768, 16), 768), :]
    done(half, c_recv)

    keys = mm(events[...], w[0]).astype(BF16)
    values = mm(events[...], w[1]).astype(BF16)
    queries = mm(normed, w[2]).astype(BF16)
    visible = iota((128, 128), 1) < len_in[0:1, :]
    low = iota((128, 128), 1) < HEAD
    mixed = []
    for pair in range(OWN // 128):
        cols = slice(128 * pair, 128 * pair + 128)
        q, k, v = queries[:, cols], keys[:, cols], values[:, cols]
        outs = []
        for mask in (low, jnp.logical_not(low)):
            scores = mm_nt(jnp.where(mask, q, jnp.zeros_like(q)), k) * HEAD ** -0.5
            scores = jnp.where(visible, scores, -1e30)
            weights = jnp.exp(scores - jnp.max(scores, axis=-1, keepdims=True))
            probs = (weights / jnp.sum(weights, axis=-1, keepdims=True)).astype(BF16)
            outs.append(mm(probs, v))
        mixed.append(jnp.where(low, outs[0], outs[1]).astype(BF16))
    mixed = jnp.concatenate(mixed, axis=1)
    part[...] = mm_nt(mixed, w[3]).astype(BF16).reshape(4, ROWS, D)

    for level in range(4):
        own = jnp.logical_and(straight, me.role == level)
        put_or_keep(own, part.at[level], parts.at[me.y], o_send.at[level], o_recv.at[me.y],
                    me.to(y_hi=me.core, y_lo=level // 2, core=level % 2))
    for k in range(4):
        done(parts.at[k], o_recv.at[k])
    attended = parts[0].astype(F32) + parts[1].astype(F32) + parts[2].astype(F32) + parts[3].astype(F32)
    hidden = (emb[...].astype(F32) + attended).astype(BF16).astype(F32)
    moe_in = norm_rows(hidden, moe_gain[...].reshape(1, D))
    packed[...] = mm(placing, moe_in).astype(BF16)

    def cut(ref, k):
        return ref.at[pl.ds(pl.multiple_of(k * 16, 16), 16), :]

    pltpu.make_async_copy(cut(packed, col), cut(got_y, col), y_recv.at[col]).start()
    for k in range(1, 8):
        d = (col + k) % 8
        put(cut(packed, d), cut(got_y, col), y_send.at[k], y_recv.at[col], in_column(d))

    logits = mm_nt(moe_in, router_t[...])
    lanes = iota(logits.shape, 1)
    picked = [
        jnp.sum(jnp.where(routes[:, k : k + 1] == lanes, logits, 0.0), axis=-1, keepdims=True)
        for k in range(2)
    ]
    top = jnp.maximum(picked[0], picked[1])
    powers = [jnp.exp(p - top) for p in picked]
    gates = [p / (powers[0] + powers[1]) for p in powers]

    for k in range(8):
        done(cut(got_y, k), y_recv.at[k])
    o, i = iota((128, 128), 0), iota((128, 128), 1)
    source = ((o // 2) % 8) * 16 + (o % 2) * 8 + o // 16
    sorted_z[...] = mm((source == i).astype(BF16), got_y[...]).astype(BF16)

    def pair_below(n, z):
        return (zp + 8 - n + 2 * n * z) % 8

    def send_z(n):
        if n:
            for first, p in ((0, (zp + n) % 8), (1, (zp + 8 - n) % 8)):
                put(cut(sorted_z, p), rows.at[n, me.x, first, pl.ds(16 * z_lo, 16), :],
                    z_send.at[n, first], z_recv.at[n, z_lo], me.to(z=p * 2 + first))
        else:
            p = (zp + 4) % 8
            put(cut(sorted_z, p), rows.at[0, me.x, 1 - z_lo, pl.ds(16, 16), :],
                z_send.at[0, 1], z_recv.at[0, 1], me.to(z=p * 2 + 1 - z_lo))
            pltpu.make_async_copy(
                cut(sorted_z, zp), rows.at[0, me.x, z_lo, pl.ds(0, 16), :], z_recv.at[0, 0]).start()

    def share_own(n):
        mine = rows.at[n, me.x, z_lo]
        for h in range(2):
            done(rows.at[n, me.x, z_lo, pl.ds(16 * h, 16), :], z_recv.at[n, h])
        put(mine, mine, p_send.at[n], p_recv.at[n], mate)
        put(mine, mine, g_send.at[n, 0, z_lo], g_recv.at[n, 0, z_lo], up)
        put(mine, mine, g_send.at[n, 1, z_lo], g_recv.at[n, 1, z_lo], down)

    def share_mate(n):
        theirs = rows.at[n, me.x, 1 - z_lo]
        done(theirs, p_recv.at[n])
        put(theirs, theirs, g_send.at[n, 0, 1 - z_lo], g_recv.at[n, 0, 1 - z_lo], up)
        put(theirs, theirs, g_send.at[n, 1, 1 - z_lo], g_recv.at[n, 1, 1 - z_lo], down)

    def relay(n):
        first, second = rows.at[n, x_down, 0], rows.at[n, x_up, 1]
        done(first, g_recv.at[n, 0, 0])
        put(first, first, r_send.at[n, 0], r_recv.at[n, 0], up)
        done(second, g_recv.at[n, 1, 1])
        put(second, second, r_send.at[n, 1], r_recv.at[n, 1], down)
        done(rows.at[n, x_down, 1], g_recv.at[n, 0, 1])
        done(rows.at[n, x_up, 0], g_recv.at[n, 1, 0])

    def apply(n):
        for b in range(2):
            done(rows.at[n, x_far, b], r_recv.at[n, b])
        if n == ORDER[0]:
            for k, dst in enumerate((wg, wu, wd)):
                done(dst, w_sem.at[k])
        here = rows[n].reshape(256, D)
        gate, lift = mm(here, wg[...]), mm(here, wu[...])
        inner = (gate / (1.0 + jnp.exp(-gate)) * lift).astype(BF16)
        res[n] = mm(inner, wd[...]).astype(BF16).reshape(4, 2, 32, D)
        put(res.at[n, x_far, 0], halves.at[n, 0], h_send.at[n, 0], h_recv.at[n, 0], up)
        put(res.at[n, x_far, 1], halves.at[n, 1], h_send.at[n, 1], h_recv.at[n, 1], down)

    def add_halves(n):
        for b, x, to in ((0, x_up, up), (1, x_down, down)):
            done(halves.at[n, b], h_recv.at[n, b])
            res[n, x, b] = (res[n, x, b].astype(F32) + halves[n, b].astype(F32)).astype(BF16)
            put(res.at[n, x], sums.at[n, b], s_send.at[n, b], s_recv.at[n, b], to)

    def total(n, z):
        return res[n, me.x, z].astype(F32) + sums[n, 0, z].astype(F32) + sums[n, 1, z].astype(F32)

    def add_x(n):
        for b in range(2):
            done(sums.at[n, b], s_recv.at[n, b])
        z_out[n] = total(n, 1 - z_lo).astype(BF16)
        put(z_out.at[n], z_in.at[n], q_send.at[n], q_recv.at[n], mate)

    def add_mate(n):
        done(z_in.at[n], q_recv.at[n])
        fin[n] = (total(n, z_lo) + z_in[n].astype(F32)).astype(BF16)
        halves_of = [fin.at[n, pl.ds(16 * h, 16), :] for h in range(2)]
        if n:
            p = pair_below(n, z_lo)
            for h in range(2):
                put(halves_of[h], cut(back_z, zp), bz_send.at[n, h], bz_recv.at[n, z_lo], me.to(z=p * 2 + h))
        else:
            pltpu.make_async_copy(halves_of[0], cut(back_z, zp), bz_recv.at[0, 0]).start()
            p = (zp + 4) % 8
            put(halves_of[1], cut(back_z, zp), bz_send.at[0, 1], bz_recv.at[0, 1], me.to(z=p * 2 + 1 - z_lo))

    def run(stages):
        for tick in range(CHUNKS + max(begin for _, begin in stages)):
            for stage, begin in stages:
                if 0 <= tick - begin < CHUNKS:
                    stage(ORDER[tick - begin])

    run(((send_z, 0), (share_own, LEAD), (share_mate, LEAD + FORWARD[0]), (relay, LEAD + FORWARD[1])))
    run(((apply, 0), (add_halves, BACKWARD[0]), (add_x, BACKWARD[1]), (add_mate, BACKWARD[2])))

    for n in range(CHUNKS):
        if n:
            done(cut(back_z, (zp + n) % 8), bz_recv.at[n, 0])
            done(cut(back_z, (zp + 8 - n) % 8), bz_recv.at[n, 1])
        else:
            done(cut(back_z, zp), bz_recv.at[0, 0])
            done(cut(back_z, (zp + 4) % 8), bz_recv.at[0, 1])
    source = (o % 8) * 16 + (o // 16) * 2 + (o // 8) % 2
    sorted_y[...] = mm((source == i).astype(BF16), back_z[...]).astype(BF16)
    pltpu.make_async_copy(cut(sorted_y, col), cut(back_y, col), by_recv.at[col]).start()
    for k in range(1, 8):
        d = (col + k) % 8
        put(cut(sorted_y, d), cut(back_y, col), by_send.at[k], by_recv.at[col], in_column(d))
    for k in range(8):
        done(cut(back_y, k), by_recv.at[k])

    chosen = gates[0] * mm(taking[0], back_y[...]) + gates[1] * mm(taking[1], back_y[...])
    out[...] = (hidden + chosen).astype(BF16)

    all_left()


def dma(*shape):
    return pltpu.SemaphoreType.DMA(shape)


def vmem(*shape, dtype=BF16):
    return pltpu.VMEM(shape, dtype)


VM = pl.BlockSpec(memory_space=pltpu.VMEM)
SM = pl.BlockSpec(memory_space=pltpu.SMEM)
HB = pl.BlockSpec(memory_space=pltpu.HBM)
ONE = pltpu.SemaphoreType.DMA


def shards(history, lengths, beam_ids, routes, code_table, w_key, w_value, w_query, w_out,
           norm_gain, moe_gain, w_router, w_gate, w_up, w_down):
    n = CHUNKS
    result = pl.pallas_call(
        layer_kernel,
        out_shape=jax.ShapeDtypeStruct((ROWS, D), BF16),
        in_specs=[VM, SM] + [VM] * 8 + [HB] * 5,
        out_specs=VM,
        scratch_shapes=[
            vmem(256, D), vmem(ROWS, D), vmem(4, ROWS, D), vmem(128, D),
            vmem(8, 128, dtype=I32), vmem(8, 128, dtype=I32),
            vmem(48, OWN), vmem(4, 16, 48, OWN), vmem(4, D, OWN), vmem(4, ROWS, D), vmem(4, ROWS, D),
            vmem(D, OWN), vmem(D, OWN), vmem(OWN, D), vmem(128, D), vmem(128, D), vmem(128, D),
            vmem(n, 4, 2, 32, D), vmem(n, 4, 2, 32, D), vmem(n, 2, 32, D), vmem(n, 2, 2, 32, D),
            vmem(n, 32, D), vmem(n, 32, D), vmem(n, 32, D), vmem(128, D), vmem(128, D), vmem(128, D),
            ONE, dma(3), ONE, ONE, dma(4), dma(4), dma(2), dma(2),
            dma(8), dma(8), dma(8), dma(8), dma(16, 2), dma(16, 2), dma(16), dma(16), dma(16), ONE, dma(4), dma(4),
            dma(8), dma(8), dma(n, 2), dma(n, 2), dma(n), dma(n), dma(n, 2, 2), dma(n, 2, 2), dma(n, 2), dma(n, 2),
            dma(n, 2), dma(n, 2), dma(n, 2), dma(n, 2), dma(n), dma(n), dma(n, 2), dma(n, 2), dma(8), dma(8),
        ],
        compiler_params=pltpu.CompilerParams(
            collective_id=0, has_side_effects=True, vmem_limit_bytes=56 * 1024 * 1024
        ),
        name="layer",
    )(beam_ids.reshape(1, ROWS), lengths, routes.reshape(ROWS, 2).T, norm_gain, moe_gain,
      w_key, w_value, w_query, w_out.T, w_router.T, code_table, history[0], w_gate[0], w_up[0], w_down[0])
    return result.reshape(1, 1, ROWS, D)


def solution(mesh):
    return jax.shard_map(
        shards,
        mesh=mesh,
        in_specs=(
            P("shard", None, None),
            P("shard"),
            P("shard", "role", None),
            P("shard", "role", None, None),
            P("role", None),
            P("shard", "role"),
            P("shard", "role"),
            P("shard", "role"),
            P("role", "shard"),
            P(),
            P(),
            P(),
            P(("role", "shard"), None, None),
            P(("role", "shard"), None, None),
            P(("role", "shard"), None, None),
        ),
        out_specs=P("shard", "role", None, None),
        check_vma=False,
    )
```

```python
import functools

import jax
import jax.numpy as jnp
from jax import lax
from jax.experimental import pallas as pl
from jax.experimental.pallas import tpu as pltpu
from jax.sharding import PartitionSpec as P

MESH = pl.DeviceIdType.MESH
F32, BF16, I32 = jnp.float32, jnp.bfloat16, jnp.int32
D = 1536
HEAD = 64
OWN = 384
ROWS = 32
EPS = 1e-06


class Here:
    def __init__(self):
        role, shard = lax.axis_index("role"), lax.axis_index("shard")
        self.role = role
        self.y_lo, self.core = role // 2, role % 2
        self.y_hi, self.z, self.x = shard // 64, (shard // 4) % 16, shard % 4
        self.y = self.y_hi * 2 + self.y_lo

    def to(self, y_hi=None, y_lo=None, core=None, z=None, x=None):
        pick = lambda new, old: old if new is None else new
        y_hi, y_lo, core = pick(y_hi, self.y_hi), pick(y_lo, self.y_lo), pick(core, self.core)
        z, x = pick(z, self.z), pick(x, self.x)
        return (y_lo * 2 + core, y_hi * 64 + z * 4 + x)


def done(ref, sem):
    pltpu.make_async_copy(ref, ref, sem).wait()


def norm_rows(values, gain):
    power = jnp.mean(values * values, axis=-1, keepdims=True)
    return (values * lax.rsqrt(power + EPS) * gain).astype(BF16)


def mm(a, b):
    return jnp.dot(a, b, preferred_element_type=F32)


def mm_nt(a, b):
    return lax.dot_general(a, b, (((1,), (1,)), ((), ())), preferred_element_type=F32)


def iota(shape, dim):
    return lax.broadcasted_iota(I32, shape, dim)


ORDER = (0, 2, 4, 5, 6, 1, 7, 3)
Z_ORDER = (1, 2, 0, 3)
CHUNKS = len(ORDER)
BEGIN = (0, 1, 2, 3, 4, 5, 6)
LAG = (2, 4)
DIRECT_FROM = 6


def layer_kernel(
    ids, lens, routes_t, gain, moe_gain, w_key, w_value, w_query, w_out_t, router_t, table_hbm, hist,
    wg_hbm, wu_hbm, wd_hbm,
    out,
    table, emb, every, events, len_out, len_in, piece, raw, w, part, parts,
    wg, wu, wd, packed, got_y, sorted_z, rows, res, halves, sums, z_out, z_in, fin, back_z, sorted_y, back_y,
    t_sem, w_sem, m_send, m_recv, e_send, e_recv, hi_send, hi_recv, f_send, f_recv, b_send, b_recv,
    d_send, d_recv, l_send, l_recv, c_send, c_recv, o_send, o_recv,
    y_send, y_recv, z_send, z_recv, p_send, p_recv, g_send, g_recv, r_send, r_recv,
    h_send, h_recv, s_send, s_recv, q_send, q_recv, bz_send, bz_recv, by_send, by_recv,
):
    me = Here()
    sent = []

    def put(src, dst, send, recv, to, listed=True):
        pltpu.make_async_remote_copy(
            src_ref=src, dst_ref=dst, send_sem=send, recv_sem=recv, device_id=to, device_id_type=MESH
        ).start()
        if listed:
            sent.append((src, send, None))

    def put_or_keep(is_self, src, dst, send, recv, to):
        @pl.when(is_self)
        def _():
            pltpu.make_async_copy(src, dst, recv).start()

        @pl.when(jnp.logical_not(is_self))
        def _():
            put(src, dst, send, recv, to, listed=False)

        sent.append((src, send, is_self))

    def all_left():
        for src, send, is_self in sent:
            if is_self is None:
                done(src, send)
            else:
                pl.when(jnp.logical_not(is_self))(functools.partial(done, src, send))

    straight = me.y_hi == me.core
    zp, z_lo = me.z // 2, me.z % 2
    col = me.y_lo * 4 + me.core * 2 + me.y_hi

    def in_column(d):
        return me.to(y_lo=d // 4, core=(d // 2) % 2, y_hi=d % 2)

    mirror = me.to(y_hi=me.core, core=me.y_hi)
    other = me.to(core=1 - me.core)
    z_up, z_down = me.to(z=(me.z + 1) % 16), me.to(z=(me.z + 15) % 16)
    mate = me.to(z=zp * 2 + 1 - z_lo)
    x_up, x_far, x_down = [(me.x + k) % 4 for k in (1, 2, 3)]
    up, far, down = me.to(x=x_up), me.to(x=x_far), me.to(x=x_down)
    partners = [in_column((col + k) % 8) for k in range(1, 8)] + [z_up, z_down, up, far, down]
    barrier = pltpu.get_barrier_semaphore()
    for to in partners:
        pl.semaphore_signal(barrier, inc=1, device_id=to, device_id_type=MESH)

    pltpu.make_async_copy(table_hbm, table, t_sem).start()
    for k, (src, dst) in enumerate(((wg_hbm, wg), (wu_hbm, wu), (wd_hbm, wd))):
        pltpu.make_async_copy(src, dst, w_sem.at[k]).start()

    o, i = iota((48, 12), 0), iota((48, 12), 1)
    stacked = jnp.zeros((48, OWN), F32)
    for m, ref in enumerate((w_key, w_value, w_query, w_out_t)):
        stacked += mm((o == i + 12 * m).astype(BF16), ref[...])
    piece[...] = stacked.astype(BF16)
    len_out[...] = jnp.full((8, 128), lens[0], I32)
    eye = (iota((ROWS, ROWS), 0) == iota((ROWS, ROWS), 1)).astype(BF16)
    lookup = mm_nt(eye, (iota((256, ROWS), 0) == ids[...]).astype(BF16)).astype(BF16)
    done(table, t_sem)
    emb[...] = mm(lookup, table[...]).astype(BF16)

    pl.semaphore_wait(barrier, len(partners))

    put_or_keep(straight, piece, raw.at[me.x, me.z], m_send, m_recv, mirror)

    o, i = iota((192, 192), 0), iota((192, 192), 1)
    ordering = (((o % 48) // 12) * 48 + (o // 48) * 12 + o % 12 == i).astype(BF16)

    def block(z):
        return w.at[:, pl.ds(pl.multiple_of(me.core * 768 + z * 48, 16), 48), :]

    def z_of(n):
        return (me.z + 16 - n) % 16 if n < 8 else (me.z + n - 7) % 16

    def share(n):
        mine = raw.at[me.x, z_of(n)]
        put(mine, mine, d_send.at[n, 0], d_recv.at[n, 0], up)
        put(mine, mine, d_send.at[n, 1], d_recv.at[n, 1], down)
        if direct(n):
            put(mine, mine, l_send.at[n], l_recv.at[n], far)

    def direct(n):
        return (n if n < 8 else n - 7) >= DIRECT_FROM

    def pass_on(n):
        z = z_of(n)
        low, high = raw.at[x_down, z], raw.at[x_up, z]
        done(low, d_recv.at[n, 0])
        if n < 8 and not direct(n):
            put(low, low, l_send.at[n], l_recv.at[n], up)
        done(high, d_recv.at[n, 1])
        if n >= 8 and not direct(n):
            put(high, high, l_send.at[n], l_recv.at[n], down)

    def settle(n):
        z = z_of(n)
        done(raw.at[x_far, z], l_recv.at[n])
        pieces = jnp.concatenate([raw[x, z] for x in range(4)], axis=0)
        block(z)[...] = mm(ordering, pieces).astype(BF16).reshape(4, 48, OWN)
        put(block(z), block(z), c_send.at[n], c_recv, other)

    own_piece = raw.at[me.x, me.z]
    done(own_piece, m_recv)
    put(own_piece, own_piece, f_send.at[0], f_recv.at[0], z_up)
    put(own_piece, own_piece, b_send.at[0], b_recv.at[0], z_down)
    share(0)

    for k in range(4):
        y = (me.y + k) % 4
        args = (emb, every.at[me.role], e_send.at[k], e_recv.at[me.role],
                me.to(y_hi=y // 2, y_lo=y % 2, core=me.y_hi))
        if k:
            put(*args)
        else:
            put_or_keep(straight, *args)

    put_or_keep(straight, hist, events, hi_send.at[0], hi_recv.at[0], mirror)
    put_or_keep(straight, len_out, len_in, hi_send.at[1], hi_recv.at[1], mirror)

    def slots(shape, dim):
        slot = iota(shape, dim)
        return (slot // 16) * 8 + slot % 8, (slot // 8) % 2

    routes = mm_nt(eye, routes_t[...].astype(BF16)).astype(I32)
    expert, order = slots((128, ROWS), 0)
    named = jnp.logical_or(routes_t[0:1, :] == expert, routes_t[1:2, :] == expert)
    earlier = (iota((ROWS, ROWS), 0) < iota((ROWS, ROWS), 1)).astype(BF16)
    before = mm(named.astype(BF16), earlier)
    placing = jnp.logical_and(named, before == order.astype(F32)).astype(BF16)
    expert_l, order_l = slots((ROWS, 128), 1)
    member = [routes[:, k : k + 1] == expert_l for k in range(2)]
    later = (iota((ROWS, ROWS), 1) < iota((ROWS, ROWS), 0)).astype(BF16)
    before_l = mm(later, jnp.logical_or(member[0], member[1]).astype(BF16))
    taking = [jnp.logical_and(m, before_l == order_l.astype(F32)).astype(BF16) for m in member]

    def lagging(stage, t):
        if t == 0:
            stage(0)
        elif 0 < t < 8:
            stage(t)
            stage(t + 7)
        elif t == 8:
            stage(15)

    for t in range(1, 9 + LAG[1]):
        if t < 9:
            for n, send, recv, to in ((t, f_send, f_recv, z_up), (t + 7, b_send, b_recv, z_down)):
                if t == 8 and n == 8:
                    continue
                ref = raw.at[me.x, z_of(n)]
                done(ref, recv.at[t - 1])
                if t < 7 or (t == 7 and n == 14):
                    put(ref, ref, send.at[t], recv.at[t], to)
                share(n)
        lagging(pass_on, t - LAG[0])
        lagging(settle, t - LAG[1])

    for k in range(4):
        done(every.at[k], e_recv.at[k])
    normed = norm_rows(every[...].reshape(4 * ROWS, D).astype(F32), gain[...].reshape(1, D))
    done(events, hi_recv.at[0])
    done(len_in, hi_recv.at[1])
    half = w.at[:, pl.ds(pl.multiple_of((1 - me.core) * 768, 16), 768), :]
    done(half, c_recv)

    keys = mm(events[...], w[0]).astype(BF16)
    values = mm(events[...], w[1]).astype(BF16)
    queries = mm(normed, w[2]).astype(BF16)
    visible = iota((128, 128), 1) < len_in[0:1, :]
    low = iota((128, 128), 1) < HEAD
    mixed = []
    for pair in range(OWN // 128):
        cols = slice(128 * pair, 128 * pair + 128)
        q, k, v = queries[:, cols], keys[:, cols], values[:, cols]
        outs = []
        for mask in (low, jnp.logical_not(low)):
            scores = mm_nt(jnp.where(mask, q, jnp.zeros_like(q)), k) * HEAD ** -0.5
            scores = jnp.where(visible, scores, -1e30)
            weights = jnp.exp(scores - jnp.max(scores, axis=-1, keepdims=True))
            probs = (weights / jnp.sum(weights, axis=-1, keepdims=True)).astype(BF16)
            outs.append(mm(probs, v))
        mixed.append(jnp.where(low, outs[0], outs[1]).astype(BF16))
    mixed = jnp.concatenate(mixed, axis=1)
    part[...] = mm_nt(mixed, w[3]).astype(BF16).reshape(4, ROWS, D)

    for level in range(4):
        own = jnp.logical_and(straight, me.role == level)
        put_or_keep(own, part.at[level], parts.at[me.y], o_send.at[level], o_recv.at[me.y],
                    me.to(y_hi=me.core, y_lo=level // 2, core=level % 2))
    for k in range(4):
        done(parts.at[k], o_recv.at[k])
    attended = parts[0].astype(F32) + parts[1].astype(F32) + parts[2].astype(F32) + parts[3].astype(F32)
    hidden = (emb[...].astype(F32) + attended).astype(BF16).astype(F32)
    moe_in = norm_rows(hidden, moe_gain[...].reshape(1, D))
    packed[...] = mm(placing, moe_in).astype(BF16)

    def cut(ref, k):
        return ref.at[pl.ds(pl.multiple_of(k * 16, 16), 16), :]

    pltpu.make_async_copy(cut(packed, col), cut(got_y, col), y_recv.at[col]).start()
    for k in range(1, 8):
        d = (col + k) % 8
        put(cut(packed, d), cut(got_y, col), y_send.at[k], y_recv.at[col], in_column(d))

    logits = mm_nt(moe_in, router_t[...])
    lanes = iota(logits.shape, 1)
    picked = [
        jnp.sum(jnp.where(routes[:, k : k + 1] == lanes, logits, 0.0), axis=-1, keepdims=True)
        for k in range(2)
    ]
    top = jnp.maximum(picked[0], picked[1])
    powers = [jnp.exp(p - top) for p in picked]
    gates = [p / (powers[0] + powers[1]) for p in powers]

    for k in range(8):
        done(cut(got_y, k), y_recv.at[k])
    o, i = iota((128, 128), 0), iota((128, 128), 1)
    source = ((o // 2) % 8) * 16 + (o % 2) * 8 + o // 16
    sorted_z[...] = mm((source == i).astype(BF16), got_y[...]).astype(BF16)

    def send_z():
        own = rows.at[0, me.x, z_lo]
        pltpu.make_async_copy(cut(sorted_z, zp), own, z_recv.at[0]).start()
        for n in Z_ORDER:
            if n:
                for first, p, s in ((0, (zp + n) % 8, 1 - z_lo), (1, (zp + 8 - n) % 8, z_lo)):
                    put(cut(sorted_z, p), rows.at[2 * n + s, me.x, first],
                        z_send.at[2 * n + first], z_recv.at[2 * n + s], me.to(z=p * 2 + first))
            else:
                p = (zp + 4) % 8
                put(cut(sorted_z, p), rows.at[1, me.x, 1 - z_lo], z_send.at[1], z_recv.at[1], me.to(z=p * 2 + 1 - z_lo))

    def share_own(q):
        mine = rows.at[q, me.x, z_lo]
        done(mine, z_recv.at[q])
        put(mine, mine, p_send.at[q], p_recv.at[q], mate)
        put(mine, mine, g_send.at[q, 0, z_lo], g_recv.at[q, 0, z_lo], up)
        put(mine, mine, g_send.at[q, 1, z_lo], g_recv.at[q, 1, z_lo], down)

    def share_mate(q):
        theirs = rows.at[q, me.x, 1 - z_lo]
        done(theirs, p_recv.at[q])
        put(theirs, theirs, g_send.at[q, 0, 1 - z_lo], g_recv.at[q, 0, 1 - z_lo], up)
        put(theirs, theirs, g_send.at[q, 1, 1 - z_lo], g_recv.at[q, 1, 1 - z_lo], down)

    def relay(q):
        first, second = rows.at[q, x_down, 0], rows.at[q, x_up, 1]
        done(first, g_recv.at[q, 0, 0])
        put(first, first, r_send.at[q, 0], r_recv.at[q, 0], up)
        done(second, g_recv.at[q, 1, 1])
        put(second, second, r_send.at[q, 1], r_recv.at[q, 1], down)
        done(rows.at[q, x_down, 1], g_recv.at[q, 0, 1])
        done(rows.at[q, x_up, 0], g_recv.at[q, 1, 0])

    def apply(q):
        for b in range(2):
            done(rows.at[q, x_far, b], r_recv.at[q, b])
        if q == ORDER[0]:
            for k, dst in enumerate((wg, wu, wd)):
                done(dst, w_sem.at[k])
        here = rows[q].reshape(128, D)
        gate, lift = mm(here, wg[...]), mm(here, wu[...])
        inner = (gate / (1.0 + jnp.exp(-gate)) * lift).astype(BF16)
        res[q] = mm(inner, wd[...]).astype(BF16).reshape(4, 2, 16, D)
        put(res.at[q, x_far, 0], halves.at[q, 0], h_send.at[q, 0], h_recv.at[q, 0], up)
        put(res.at[q, x_far, 1], halves.at[q, 1], h_send.at[q, 1], h_recv.at[q, 1], down)

    def add_halves(q):
        for b, x, to in ((0, x_up, up), (1, x_down, down)):
            done(halves.at[q, b], h_recv.at[q, b])
            res[q, x, b] = (res[q, x, b].astype(F32) + halves[q, b].astype(F32)).astype(BF16)
            put(res.at[q, x], sums.at[q, b], s_send.at[q, b], s_recv.at[q, b], to)

    def total(q, z):
        return res[q, me.x, z].astype(F32) + sums[q, 0, z].astype(F32) + sums[q, 1, z].astype(F32)

    def add_x(q):
        for b in range(2):
            done(sums.at[q, b], s_recv.at[q, b])
        z_out[q] = total(q, 1 - z_lo).astype(BF16)
        put(z_out.at[q], z_in.at[q], q_send.at[q], q_recv.at[q], mate)

    def add_mate(q):
        done(z_in.at[q], q_recv.at[q])
        fin[q] = (total(q, z_lo) + z_in[q].astype(F32)).astype(BF16)
        n, s = q // 2, q % 2
        if n:
            p = (zp + 8 - n + 2 * n * z_lo) % 8
            to = me.to(z=p * 2 + (1 - s) * (1 - z_lo) + s * z_lo)
            put(fin.at[q], cut(back_z, zp), bz_send.at[q], bz_recv.at[2 * n + z_lo], to)
        elif s:
            p = (zp + 4) % 8
            put(fin.at[1], cut(back_z, zp), bz_send.at[1], bz_recv.at[1], me.to(z=p * 2 + 1 - z_lo))
        else:
            pltpu.make_async_copy(fin.at[0], cut(back_z, zp), bz_recv.at[0]).start()

    def run(stages):
        for tick in range(CHUNKS + max(begin for _, begin in stages)):
            for stage, begin in stages:
                if 0 <= tick - begin < CHUNKS:
                    stage(ORDER[tick - begin])

    send_z()
    run(list(zip((share_own, share_mate, relay, apply, add_halves, add_x, add_mate), BEGIN)))

    for n in range(4):
        if n:
            done(cut(back_z, (zp + n) % 8), bz_recv.at[2 * n])
            done(cut(back_z, (zp + 8 - n) % 8), bz_recv.at[2 * n + 1])
        else:
            done(cut(back_z, zp), bz_recv.at[0])
            done(cut(back_z, (zp + 4) % 8), bz_recv.at[1])
    source = (o % 8) * 16 + (o // 16) * 2 + (o // 8) % 2
    sorted_y[...] = mm((source == i).astype(BF16), back_z[...]).astype(BF16)
    pltpu.make_async_copy(cut(sorted_y, col), cut(back_y, col), by_recv.at[col]).start()
    for k in range(1, 8):
        d = (col + k) % 8
        put(cut(sorted_y, d), cut(back_y, col), by_send.at[k], by_recv.at[col], in_column(d))
    for k in range(8):
        done(cut(back_y, k), by_recv.at[k])

    chosen = gates[0] * mm(taking[0], back_y[...]) + gates[1] * mm(taking[1], back_y[...])
    out[...] = (hidden + chosen).astype(BF16)

    all_left()


def dma(*shape):
    return pltpu.SemaphoreType.DMA(shape)


def vmem(*shape, dtype=BF16):
    return pltpu.VMEM(shape, dtype)


VM = pl.BlockSpec(memory_space=pltpu.VMEM)
SM = pl.BlockSpec(memory_space=pltpu.SMEM)
HB = pl.BlockSpec(memory_space=pltpu.HBM)
ONE = pltpu.SemaphoreType.DMA


def shards(history, lengths, beam_ids, routes, code_table, w_key, w_value, w_query, w_out,
           norm_gain, moe_gain, w_router, w_gate, w_up, w_down):
    n = CHUNKS
    result = pl.pallas_call(
        layer_kernel,
        out_shape=jax.ShapeDtypeStruct((ROWS, D), BF16),
        in_specs=[VM, SM] + [VM] * 8 + [HB] * 5,
        out_specs=VM,
        scratch_shapes=[
            vmem(256, D), vmem(ROWS, D), vmem(4, ROWS, D), vmem(128, D),
            vmem(8, 128, dtype=I32), vmem(8, 128, dtype=I32),
            vmem(48, OWN), vmem(4, 16, 48, OWN), vmem(4, D, OWN), vmem(4, ROWS, D), vmem(4, ROWS, D),
            vmem(D, OWN), vmem(D, OWN), vmem(OWN, D), vmem(128, D), vmem(128, D), vmem(128, D),
            vmem(n, 4, 2, 16, D), vmem(n, 4, 2, 16, D), vmem(n, 2, 16, D), vmem(n, 2, 2, 16, D),
            vmem(n, 16, D), vmem(n, 16, D), vmem(n, 16, D), vmem(128, D), vmem(128, D), vmem(128, D),
            ONE, dma(3), ONE, ONE, dma(4), dma(4), dma(2), dma(2),
            dma(8), dma(8), dma(8), dma(8), dma(16, 2), dma(16, 2), dma(16), dma(16), dma(16), ONE, dma(4), dma(4),
            dma(8), dma(8), dma(n), dma(n), dma(n), dma(n), dma(n, 2, 2), dma(n, 2, 2), dma(n, 2), dma(n, 2),
            dma(n, 2), dma(n, 2), dma(n, 2), dma(n, 2), dma(n), dma(n), dma(n), dma(n), dma(8), dma(8),
        ],
        compiler_params=pltpu.CompilerParams(
            collective_id=0, has_side_effects=True, vmem_limit_bytes=56 * 1024 * 1024
        ),
        name="layer",
    )(beam_ids.reshape(1, ROWS), lengths, routes.reshape(ROWS, 2).T, norm_gain, moe_gain,
      w_key, w_value, w_query, w_out.T, w_router.T, code_table, history[0], w_gate[0], w_up[0], w_down[0])
    return result.reshape(1, 1, ROWS, D)


def solution(mesh):
    return jax.shard_map(
        shards,
        mesh=mesh,
        in_specs=(
            P("shard", None, None),
            P("shard"),
            P("shard", "role", None),
            P("shard", "role", None, None),
            P("role", None),
            P("shard", "role"),
            P("shard", "role"),
            P("shard", "role"),
            P("role", "shard"),
            P(),
            P(),
            P(),
            P(("role", "shard"), None, None),
            P(("role", "shard"), None, None),
            P(("role", "shard"), None, None),
        ),
        out_specs=P("shard", "role", None, None),
        check_vma=False,
    )
```

```python
import functools

import jax
import jax.numpy as jnp
from jax import lax
from jax.experimental import pallas as pl
from jax.experimental.pallas import tpu as pltpu
from jax.sharding import PartitionSpec as P

MESH = pl.DeviceIdType.MESH
F32, BF16, I32 = jnp.float32, jnp.bfloat16, jnp.int32
D = 1536
HEAD = 64
OWN = 384
ROWS = 32
EPS = 1e-06


class Here:
    def __init__(self):
        role, shard = lax.axis_index("role"), lax.axis_index("shard")
        self.role = role
        self.y_lo, self.core = role // 2, role % 2
        self.y_hi, self.z, self.x = shard // 64, (shard // 4) % 16, shard % 4
        self.y = self.y_hi * 2 + self.y_lo

    def to(self, y_hi=None, y_lo=None, core=None, z=None, x=None):
        pick = lambda new, old: old if new is None else new
        y_hi, y_lo, core = pick(y_hi, self.y_hi), pick(y_lo, self.y_lo), pick(core, self.core)
        z, x = pick(z, self.z), pick(x, self.x)
        return (y_lo * 2 + core, y_hi * 64 + z * 4 + x)


def done(ref, sem):
    pltpu.make_async_copy(ref, ref, sem).wait()


def norm_rows(values, gain):
    power = jnp.mean(values * values, axis=-1, keepdims=True)
    return (values * lax.rsqrt(power + EPS) * gain).astype(BF16)


def mm(a, b):
    return jnp.dot(a, b, preferred_element_type=F32)


def mm_nt(a, b):
    return lax.dot_general(a, b, (((1,), (1,)), ((), ())), preferred_element_type=F32)


def iota(shape, dim):
    return lax.broadcasted_iota(I32, shape, dim)


ORDER = (0, 2, 4, 5, 6, 1, 7, 3)
Z_ORDER = (1, 2, 0, 3)
CHUNKS = len(ORDER)
BEGIN = (0, 1, 2, 3, 4, 5, 6)
LAG = (2, 4)
DIRECT_FROM = 6


def layer_kernel(
    ids, lens, routes_t, gain, moe_gain, w_key, w_value, w_query, w_out_t, router_t, table_hbm, hist,
    wg_hbm, wu_hbm, wd_hbm,
    out,
    table, emb, every, events, len_out, len_in, piece, raw, w, part, parts,
    wg, wu, wd, packed, got_y, sorted_z, rows, res, halves, sums, z_out, z_in, fin, back_z, sorted_y, back_y,
    t_sem, w_sem, m_send, m_recv, e_send, e_recv, hi_send, hi_recv, f_send, f_recv, b_send, b_recv,
    d_send, d_recv, l_send, l_recv, c_send, c_recv, o_send, o_recv,
    y_send, y_recv, z_send, z_recv, p_send, p_recv, g_send, g_recv, r_send, r_recv,
    h_send, h_recv, s_send, s_recv, q_send, q_recv, bz_send, bz_recv, by_send, by_recv,
):
    me = Here()
    sent = []

    def put(src, dst, send, recv, to, listed=True):
        pltpu.make_async_remote_copy(
            src_ref=src, dst_ref=dst, send_sem=send, recv_sem=recv, device_id=to, device_id_type=MESH
        ).start()
        if listed:
            sent.append((src, send, None))

    def put_or_keep(is_self, src, dst, send, recv, to):
        @pl.when(is_self)
        def _():
            pltpu.make_async_copy(src, dst, recv).start()

        @pl.when(jnp.logical_not(is_self))
        def _():
            put(src, dst, send, recv, to, listed=False)

        sent.append((src, send, is_self))

    def all_left(but_last=0):
        while len(sent) > but_last:
            src, send, is_self = sent.pop(0)
            if is_self is None:
                done(src, send)
            else:
                pl.when(jnp.logical_not(is_self))(functools.partial(done, src, send))

    straight = me.y_hi == me.core
    zp, z_lo = me.z // 2, me.z % 2
    col = me.y_lo * 4 + me.core * 2 + me.y_hi

    def in_column(d):
        return me.to(y_lo=d // 4, core=(d // 2) % 2, y_hi=d % 2)

    mirror = me.to(y_hi=me.core, core=me.y_hi)
    other = me.to(core=1 - me.core)
    z_up, z_down = me.to(z=(me.z + 1) % 16), me.to(z=(me.z + 15) % 16)
    mate = me.to(z=zp * 2 + 1 - z_lo)
    x_up, x_far, x_down = [(me.x + k) % 4 for k in (1, 2, 3)]
    up, far, down = me.to(x=x_up), me.to(x=x_far), me.to(x=x_down)
    partners = [in_column((col + k) % 8) for k in range(1, 8)] + [z_up, z_down, up, far, down]
    barrier = pltpu.get_barrier_semaphore()
    for to in partners:
        pl.semaphore_signal(barrier, inc=1, device_id=to, device_id_type=MESH)

    pltpu.make_async_copy(table_hbm, table, t_sem).start()
    for k, (src, dst) in enumerate(((wg_hbm, wg), (wu_hbm, wu), (wd_hbm, wd))):
        pltpu.make_async_copy(src, dst, w_sem.at[k]).start()

    o, i = iota((48, 12), 0), iota((48, 12), 1)
    stacked = jnp.zeros((48, OWN), F32)
    for m, ref in enumerate((w_key, w_value, w_query, w_out_t)):
        stacked += mm((o == i + 12 * m).astype(BF16), ref[...])
    piece[...] = stacked.astype(BF16)

    pl.semaphore_wait(barrier, len(partners))

    put_or_keep(straight, piece, raw.at[me.x, me.z], m_send, m_recv, mirror)

    o, i = iota((192, 192), 0), iota((192, 192), 1)
    ordering = (((o % 48) // 12) * 48 + (o // 48) * 12 + o % 12 == i).astype(BF16)

    def block(z):
        return w.at[:, pl.ds(pl.multiple_of(me.core * 768 + z * 48, 16), 48), :]

    def z_of(n):
        return (me.z + 16 - n) % 16 if n < 8 else (me.z + n - 7) % 16

    def share(n):
        mine = raw.at[me.x, z_of(n)]
        put(mine, mine, d_send.at[n, 0], d_recv.at[n, 0], up)
        put(mine, mine, d_send.at[n, 1], d_recv.at[n, 1], down)
        if direct(n):
            put(mine, mine, l_send.at[n], l_recv.at[n], far)

    def direct(n):
        return (n if n < 8 else n - 7) >= DIRECT_FROM

    def pass_on(n):
        z = z_of(n)
        low, high = raw.at[x_down, z], raw.at[x_up, z]
        done(low, d_recv.at[n, 0])
        if n < 8 and not direct(n):
            put(low, low, l_send.at[n], l_recv.at[n], up)
        done(high, d_recv.at[n, 1])
        if n >= 8 and not direct(n):
            put(high, high, l_send.at[n], l_recv.at[n], down)

    def settle(n):
        z = z_of(n)
        done(raw.at[x_far, z], l_recv.at[n])
        pieces = jnp.concatenate([raw[x, z] for x in range(4)], axis=0)
        block(z)[...] = mm(ordering, pieces).astype(BF16).reshape(4, 48, OWN)
        put(block(z), block(z), c_send.at[n], c_recv, other)

    own_piece = raw.at[me.x, me.z]
    done(own_piece, m_recv)
    put(own_piece, own_piece, f_send.at[0], f_recv.at[0], z_up)
    put(own_piece, own_piece, b_send.at[0], b_recv.at[0], z_down)
    share(0)

    len_out[...] = jnp.full((8, 128), lens[0], I32)
    eye = (iota((ROWS, ROWS), 0) == iota((ROWS, ROWS), 1)).astype(BF16)
    lookup = mm_nt(eye, (iota((256, ROWS), 0) == ids[...]).astype(BF16)).astype(BF16)
    done(table, t_sem)
    emb[...] = mm(lookup, table[...]).astype(BF16)

    for k in range(4):
        y = (me.y + k) % 4
        args = (emb, every.at[me.role], e_send.at[k], e_recv.at[me.role],
                me.to(y_hi=y // 2, y_lo=y % 2, core=me.y_hi))
        if k:
            put(*args)
        else:
            put_or_keep(straight, *args)

    put_or_keep(straight, hist, events, hi_send.at[0], hi_recv.at[0], mirror)
    put_or_keep(straight, len_out, len_in, hi_send.at[1], hi_recv.at[1], mirror)

    def slots(shape, dim):
        slot = iota(shape, dim)
        return (slot // 16) * 8 + slot % 8, (slot // 8) % 2

    routes = mm_nt(eye, routes_t[...].astype(BF16)).astype(I32)
    expert, order = slots((128, ROWS), 0)
    named = jnp.logical_or(routes_t[0:1, :] == expert, routes_t[1:2, :] == expert)
    earlier = (iota((ROWS, ROWS), 0) < iota((ROWS, ROWS), 1)).astype(BF16)
    before = mm(named.astype(BF16), earlier)
    placing = jnp.logical_and(named, before == order.astype(F32)).astype(BF16)
    expert_l, order_l = slots((ROWS, 128), 1)
    member = [routes[:, k : k + 1] == expert_l for k in range(2)]
    later = (iota((ROWS, ROWS), 1) < iota((ROWS, ROWS), 0)).astype(BF16)
    before_l = mm(later, jnp.logical_or(member[0], member[1]).astype(BF16))
    taking = [jnp.logical_and(m, before_l == order_l.astype(F32)).astype(BF16) for m in member]

    def lagging(stage, t):
        if t == 0:
            stage(0)
        elif 0 < t < 8:
            stage(t)
            stage(t + 7)
        elif t == 8:
            stage(15)

    for t in range(1, 9 + LAG[1]):
        if t < 9:
            for n, send, recv, to in ((t, f_send, f_recv, z_up), (t + 7, b_send, b_recv, z_down)):
                if t == 8 and n == 8:
                    continue
                ref = raw.at[me.x, z_of(n)]
                done(ref, recv.at[t - 1])
                if t < 7 or (t == 7 and n == 14):
                    put(ref, ref, send.at[t], recv.at[t], to)
                share(n)
        lagging(pass_on, t - LAG[0])
        lagging(settle, t - LAG[1])

    for k in range(4):
        done(every.at[k], e_recv.at[k])
    normed = norm_rows(every[...].reshape(4 * ROWS, D).astype(F32), gain[...].reshape(1, D))
    done(events, hi_recv.at[0])
    done(len_in, hi_recv.at[1])
    half = w.at[:, pl.ds(pl.multiple_of((1 - me.core) * 768, 16), 768), :]
    done(half, c_recv)

    keys = mm(events[...], w[0]).astype(BF16)
    values = mm(events[...], w[1]).astype(BF16)
    queries = mm(normed, w[2]).astype(BF16)
    visible = iota((128, 128), 1) < len_in[0:1, :]
    low = iota((128, 128), 1) < HEAD
    mixed = []
    for pair in range(OWN // 128):
        cols = slice(128 * pair, 128 * pair + 128)
        q, k, v = queries[:, cols], keys[:, cols], values[:, cols]
        outs = []
        for mask in (low, jnp.logical_not(low)):
            scores = mm_nt(jnp.where(mask, q, jnp.zeros_like(q)), k) * HEAD ** -0.5
            scores = jnp.where(visible, scores, -1e30)
            weights = jnp.exp(scores - jnp.max(scores, axis=-1, keepdims=True))
            probs = (weights / jnp.sum(weights, axis=-1, keepdims=True)).astype(BF16)
            outs.append(mm(probs, v))
        mixed.append(jnp.where(low, outs[0], outs[1]).astype(BF16))
    mixed = jnp.concatenate(mixed, axis=1)
    part[...] = mm_nt(mixed, w[3]).astype(BF16).reshape(4, ROWS, D)

    for level in range(4):
        own = jnp.logical_and(straight, me.role == level)
        put_or_keep(own, part.at[level], parts.at[me.y], o_send.at[level], o_recv.at[me.y],
                    me.to(y_hi=me.core, y_lo=level // 2, core=level % 2))
    for k in range(4):
        done(parts.at[k], o_recv.at[k])
    attended = parts[0].astype(F32) + parts[1].astype(F32) + parts[2].astype(F32) + parts[3].astype(F32)
    hidden = (emb[...].astype(F32) + attended).astype(BF16).astype(F32)
    moe_in = norm_rows(hidden, moe_gain[...].reshape(1, D))
    packed[...] = mm(placing, moe_in).astype(BF16)

    def cut(ref, k):
        return ref.at[pl.ds(pl.multiple_of(k * 16, 16), 16), :]

    pltpu.make_async_copy(cut(packed, col), cut(got_y, col), y_recv.at[col]).start()
    for k in range(1, 8):
        d = (col + k) % 8
        put(cut(packed, d), cut(got_y, col), y_send.at[k], y_recv.at[col], in_column(d))

    logits = mm_nt(moe_in, router_t[...])
    lanes = iota(logits.shape, 1)
    picked = [
        jnp.sum(jnp.where(routes[:, k : k + 1] == lanes, logits, 0.0), axis=-1, keepdims=True)
        for k in range(2)
    ]
    top = jnp.maximum(picked[0], picked[1])
    powers = [jnp.exp(p - top) for p in picked]
    gates = [p / (powers[0] + powers[1]) for p in powers]

    all_left(but_last=7)
    for k in range(8):
        done(cut(got_y, k), y_recv.at[k])
    o, i = iota((128, 128), 0), iota((128, 128), 1)
    source = ((o // 2) % 8) * 16 + (o % 2) * 8 + o // 16
    sorted_z[...] = mm((source == i).astype(BF16), got_y[...]).astype(BF16)

    def send_z():
        own = rows.at[0, me.x, z_lo]
        pltpu.make_async_copy(cut(sorted_z, zp), own, z_recv.at[0]).start()
        for n in Z_ORDER:
            if n:
                for first, p, s in ((0, (zp + n) % 8, 1 - z_lo), (1, (zp + 8 - n) % 8, z_lo)):
                    put(cut(sorted_z, p), rows.at[2 * n + s, me.x, first],
                        z_send.at[2 * n + first], z_recv.at[2 * n + s], me.to(z=p * 2 + first))
            else:
                p = (zp + 4) % 8
                put(cut(sorted_z, p), rows.at[1, me.x, 1 - z_lo], z_send.at[1], z_recv.at[1], me.to(z=p * 2 + 1 - z_lo))

    def share_own(q):
        mine = rows.at[q, me.x, z_lo]
        done(mine, z_recv.at[q])
        put(mine, mine, p_send.at[q], p_recv.at[q], mate)
        put(mine, mine, g_send.at[q, 0, z_lo], g_recv.at[q, 0, z_lo], up)
        put(mine, mine, g_send.at[q, 1, z_lo], g_recv.at[q, 1, z_lo], down)

    def share_mate(q):
        theirs = rows.at[q, me.x, 1 - z_lo]
        done(theirs, p_recv.at[q])
        put(theirs, theirs, g_send.at[q, 0, 1 - z_lo], g_recv.at[q, 0, 1 - z_lo], up)
        put(theirs, theirs, g_send.at[q, 1, 1 - z_lo], g_recv.at[q, 1, 1 - z_lo], down)

    def relay(q):
        first, second = rows.at[q, x_down, 0], rows.at[q, x_up, 1]
        done(first, g_recv.at[q, 0, 0])
        put(first, first, r_send.at[q, 0], r_recv.at[q, 0], up)
        done(second, g_recv.at[q, 1, 1])
        put(second, second, r_send.at[q, 1], r_recv.at[q, 1], down)
        done(rows.at[q, x_down, 1], g_recv.at[q, 0, 1])
        done(rows.at[q, x_up, 0], g_recv.at[q, 1, 0])

    def apply(q):
        for b in range(2):
            done(rows.at[q, x_far, b], r_recv.at[q, b])
        if q == ORDER[0]:
            for k, dst in enumerate((wg, wu, wd)):
                done(dst, w_sem.at[k])
        here = rows[q].reshape(128, D)
        gate, lift = mm(here, wg[...]), mm(here, wu[...])
        inner = (gate / (1.0 + jnp.exp(-gate)) * lift).astype(BF16)
        res[q] = mm(inner, wd[...]).astype(BF16).reshape(4, 2, 16, D)
        put(res.at[q, x_far, 0], halves.at[q, 0], h_send.at[q, 0], h_recv.at[q, 0], up)
        put(res.at[q, x_far, 1], halves.at[q, 1], h_send.at[q, 1], h_recv.at[q, 1], down)

    def add_halves(q):
        for b, x, to in ((0, x_up, up), (1, x_down, down)):
            done(halves.at[q, b], h_recv.at[q, b])
            res[q, x, b] = (res[q, x, b].astype(F32) + halves[q, b].astype(F32)).astype(BF16)
            put(res.at[q, x], sums.at[q, b], s_send.at[q, b], s_recv.at[q, b], to)

    def total(q, z):
        return res[q, me.x, z].astype(F32) + sums[q, 0, z].astype(F32) + sums[q, 1, z].astype(F32)

    def add_x(q):
        for b in range(2):
            done(sums.at[q, b], s_recv.at[q, b])
        z_out[q] = total(q, 1 - z_lo).astype(BF16)
        put(z_out.at[q], z_in.at[q], q_send.at[q], q_recv.at[q], mate)

    def add_mate(q):
        done(z_in.at[q], q_recv.at[q])
        fin[q] = (total(q, z_lo) + z_in[q].astype(F32)).astype(BF16)
        n, s = q // 2, q % 2
        if n:
            p = (zp + 8 - n + 2 * n * z_lo) % 8
            to = me.to(z=p * 2 + (1 - s) * (1 - z_lo) + s * z_lo)
            put(fin.at[q], cut(back_z, zp), bz_send.at[q], bz_recv.at[2 * n + z_lo], to)
        elif s:
            p = (zp + 4) % 8
            put(fin.at[1], cut(back_z, zp), bz_send.at[1], bz_recv.at[1], me.to(z=p * 2 + 1 - z_lo))
        else:
            pltpu.make_async_copy(fin.at[0], cut(back_z, zp), bz_recv.at[0]).start()

    def run(stages):
        for tick in range(CHUNKS + max(begin for _, begin in stages)):
            for stage, begin in stages:
                if 0 <= tick - begin < CHUNKS:
                    stage(ORDER[tick - begin])

    send_z()
    run(list(zip((share_own, share_mate, relay, apply, add_halves, add_x, add_mate), BEGIN)))

    for n in range(4):
        if n:
            done(cut(back_z, (zp + n) % 8), bz_recv.at[2 * n])
            done(cut(back_z, (zp + 8 - n) % 8), bz_recv.at[2 * n + 1])
        else:
            done(cut(back_z, zp), bz_recv.at[0])
            done(cut(back_z, (zp + 4) % 8), bz_recv.at[1])
    source = (o % 8) * 16 + (o // 16) * 2 + (o // 8) % 2
    sorted_y[...] = mm((source == i).astype(BF16), back_z[...]).astype(BF16)
    pltpu.make_async_copy(cut(sorted_y, col), cut(back_y, col), by_recv.at[col]).start()
    for k in range(1, 8):
        d = (col + k) % 8
        put(cut(sorted_y, d), cut(back_y, col), by_send.at[k], by_recv.at[col], in_column(d))
    all_left(but_last=7)
    for k in range(8):
        done(cut(back_y, k), by_recv.at[k])

    chosen = gates[0] * mm(taking[0], back_y[...]) + gates[1] * mm(taking[1], back_y[...])
    out[...] = (hidden + chosen).astype(BF16)

    all_left()


def dma(*shape):
    return pltpu.SemaphoreType.DMA(shape)


def vmem(*shape, dtype=BF16):
    return pltpu.VMEM(shape, dtype)


VM = pl.BlockSpec(memory_space=pltpu.VMEM)
SM = pl.BlockSpec(memory_space=pltpu.SMEM)
HB = pl.BlockSpec(memory_space=pltpu.HBM)
ONE = pltpu.SemaphoreType.DMA


def shards(history, lengths, beam_ids, routes, code_table, w_key, w_value, w_query, w_out,
           norm_gain, moe_gain, w_router, w_gate, w_up, w_down):
    n = CHUNKS
    result = pl.pallas_call(
        layer_kernel,
        out_shape=jax.ShapeDtypeStruct((ROWS, D), BF16),
        in_specs=[VM, SM] + [VM] * 8 + [HB] * 5,
        out_specs=VM,
        scratch_shapes=[
            vmem(256, D), vmem(ROWS, D), vmem(4, ROWS, D), vmem(128, D),
            vmem(8, 128, dtype=I32), vmem(8, 128, dtype=I32),
            vmem(48, OWN), vmem(4, 16, 48, OWN), vmem(4, D, OWN), vmem(4, ROWS, D), vmem(4, ROWS, D),
            vmem(D, OWN), vmem(D, OWN), vmem(OWN, D), vmem(128, D), vmem(128, D), vmem(128, D),
            vmem(n, 4, 2, 16, D), vmem(n, 4, 2, 16, D), vmem(n, 2, 16, D), vmem(n, 2, 2, 16, D),
            vmem(n, 16, D), vmem(n, 16, D), vmem(n, 16, D), vmem(128, D), vmem(128, D), vmem(128, D),
            ONE, dma(3), ONE, ONE, dma(4), dma(4), dma(2), dma(2),
            dma(8), dma(8), dma(8), dma(8), dma(16, 2), dma(16, 2), dma(16), dma(16), dma(16), ONE, dma(4), dma(4),
            dma(8), dma(8), dma(n), dma(n), dma(n), dma(n), dma(n, 2, 2), dma(n, 2, 2), dma(n, 2), dma(n, 2),
            dma(n, 2), dma(n, 2), dma(n, 2), dma(n, 2), dma(n), dma(n), dma(n), dma(n), dma(8), dma(8),
        ],
        compiler_params=pltpu.CompilerParams(
            collective_id=0, has_side_effects=True, vmem_limit_bytes=56 * 1024 * 1024
        ),
        name="layer",
    )(beam_ids.reshape(1, ROWS), lengths, routes.reshape(ROWS, 2).T, norm_gain, moe_gain,
      w_key, w_value, w_query, w_out.T, w_router.T, code_table, history[0], w_gate[0], w_up[0], w_down[0])
    return result.reshape(1, 1, ROWS, D)


def solution(mesh):
    return jax.shard_map(
        shards,
        mesh=mesh,
        in_specs=(
            P("shard", None, None),
            P("shard"),
            P("shard", "role", None),
            P("shard", "role", None, None),
            P("role", None),
            P("shard", "role"),
            P("shard", "role"),
            P("shard", "role"),
            P("role", "shard"),
            P(),
            P(),
            P(),
            P(("role", "shard"), None, None),
            P(("role", "shard"), None, None),
            P(("role", "shard"), None, None),
        ),
        out_specs=P("shard", "role", None, None),
        check_vma=False,
    )
```

```python
import functools

import jax
import jax.numpy as jnp
from jax import lax
from jax.experimental import pallas as pl
from jax.experimental.pallas import tpu as pltpu
from jax.sharding import PartitionSpec as P

MESH = pl.DeviceIdType.MESH
F32, BF16, I32 = jnp.float32, jnp.bfloat16, jnp.int32
D = 1536
HEAD = 64
OWN = 384
ROWS = 32
EPS = 1e-06


class Here:
    def __init__(self):
        role, shard = lax.axis_index("role"), lax.axis_index("shard")
        self.role = role
        self.y_lo, self.core = role // 2, role % 2
        self.y_hi, self.z, self.x = shard // 64, (shard // 4) % 16, shard % 4
        self.y = self.y_hi * 2 + self.y_lo

    def to(self, y_hi=None, y_lo=None, core=None, z=None, x=None):
        pick = lambda new, old: old if new is None else new
        y_hi, y_lo, core = pick(y_hi, self.y_hi), pick(y_lo, self.y_lo), pick(core, self.core)
        z, x = pick(z, self.z), pick(x, self.x)
        return (y_lo * 2 + core, y_hi * 64 + z * 4 + x)


def done(ref, sem):
    pltpu.make_async_copy(ref, ref, sem).wait()


def norm_rows(values, gain):
    power = jnp.mean(values * values, axis=-1, keepdims=True)
    return (values * lax.rsqrt(power + EPS) * gain).astype(BF16)


def mm(a, b):
    return jnp.dot(a, b, preferred_element_type=F32)


def mm_nt(a, b):
    return lax.dot_general(a, b, (((1,), (1,)), ((), ())), preferred_element_type=F32)


def iota(shape, dim):
    return lax.broadcasted_iota(I32, shape, dim)


ORDER = (0, 2, 4, 5, 6, 1, 7, 3)
Z_ORDER = (1, 2, 0, 3)
CHUNKS = len(ORDER)
BEGIN = (0, 1, 2, 3, 4, 5, 6)
LAG = (2, 3)
DIRECT_FROM = 5


def layer_kernel(
    ids, lens, routes_t, gain, moe_gain, w_key, w_value, w_query, w_out_t, router_t, table_hbm, hist,
    wg_hbm, wu_hbm, wd_hbm,
    out,
    table, emb, every, events, len_out, len_in, piece, raw, w, part, parts,
    wg, wu, wd, packed, got_y, sorted_z, rows, res, halves, sums, z_out, z_in, fin, back_z, sorted_y, back_y,
    t_sem, w_sem, m_send, m_recv, e_send, e_recv, hi_send, hi_recv, f_send, f_recv, b_send, b_recv,
    d_send, d_recv, l_send, l_recv, c_send, c_recv, o_send, o_recv,
    y_send, y_recv, z_send, z_recv, p_send, p_recv, g_send, g_recv, r_send, r_recv,
    h_send, h_recv, s_send, s_recv, q_send, q_recv, bz_send, bz_recv, by_send, by_recv,
):
    me = Here()
    sent = []

    def put(src, dst, send, recv, to, listed=True):
        pltpu.make_async_remote_copy(
            src_ref=src, dst_ref=dst, send_sem=send, recv_sem=recv, device_id=to, device_id_type=MESH
        ).start()
        if listed:
            sent.append((src, send, None))

    def put_or_keep(is_self, src, dst, send, recv, to):
        @pl.when(is_self)
        def _():
            pltpu.make_async_copy(src, dst, recv).start()

        @pl.when(jnp.logical_not(is_self))
        def _():
            put(src, dst, send, recv, to, listed=False)

        sent.append((src, send, is_self))

    def all_left(but_last=0):
        while len(sent) > but_last:
            src, send, is_self = sent.pop(0)
            if is_self is None:
                done(src, send)
            else:
                pl.when(jnp.logical_not(is_self))(functools.partial(done, src, send))

    straight = me.y_hi == me.core
    zp, z_lo = me.z // 2, me.z % 2
    col = me.y_lo * 4 + me.core * 2 + me.y_hi

    def in_column(d):
        return me.to(y_lo=d // 4, core=(d // 2) % 2, y_hi=d % 2)

    mirror = me.to(y_hi=me.core, core=me.y_hi)
    other = me.to(core=1 - me.core)
    z_up, z_down = me.to(z=(me.z + 1) % 16), me.to(z=(me.z + 15) % 16)
    mate = me.to(z=zp * 2 + 1 - z_lo)
    x_up, x_far, x_down = [(me.x + k) % 4 for k in (1, 2, 3)]
    up, far, down = me.to(x=x_up), me.to(x=x_far), me.to(x=x_down)
    partners = [in_column((col + k) % 8) for k in range(1, 8)] + [z_up, z_down, up, far, down]
    barrier = pltpu.get_barrier_semaphore()
    for to in partners:
        pl.semaphore_signal(barrier, inc=1, device_id=to, device_id_type=MESH)

    pltpu.make_async_copy(table_hbm, table, t_sem).start()
    for k, (src, dst) in enumerate(((wg_hbm, wg), (wu_hbm, wu), (wd_hbm, wd))):
        pltpu.make_async_copy(src, dst, w_sem.at[k]).start()

    o, i = iota((48, 12), 0), iota((48, 12), 1)
    stacked = jnp.zeros((48, OWN), F32)
    for m, ref in enumerate((w_key, w_value, w_query, w_out_t)):
        stacked += mm((o == i + 12 * m).astype(BF16), ref[...])
    piece[...] = stacked.astype(BF16)

    pl.semaphore_wait(barrier, len(partners))

    put_or_keep(straight, piece, raw.at[me.x, me.z], m_send, m_recv, mirror)

    o, i = iota((192, 192), 0), iota((192, 192), 1)
    ordering = (((o % 48) // 12) * 48 + (o // 48) * 12 + o % 12 == i).astype(BF16)

    def block(z):
        return w.at[:, pl.ds(pl.multiple_of(me.core * 768 + z * 48, 16), 48), :]

    def z_of(n):
        return (me.z + 16 - n) % 16 if n < 8 else (me.z + n - 7) % 16

    def share(n):
        mine = raw.at[me.x, z_of(n)]
        put(mine, mine, d_send.at[n, 0], d_recv.at[n, 0], up)
        put(mine, mine, d_send.at[n, 1], d_recv.at[n, 1], down)
        if direct(n):
            put(mine, mine, l_send.at[n], l_recv.at[n], far)

    def direct(n):
        return (n if n < 8 else n - 7) >= DIRECT_FROM

    def pass_on(n):
        z = z_of(n)
        low, high = raw.at[x_down, z], raw.at[x_up, z]
        done(low, d_recv.at[n, 0])
        if n < 8 and not direct(n):
            put(low, low, l_send.at[n], l_recv.at[n], up)
        done(high, d_recv.at[n, 1])
        if n >= 8 and not direct(n):
            put(high, high, l_send.at[n], l_recv.at[n], down)

    def settle(n):
        z = z_of(n)
        done(raw.at[x_far, z], l_recv.at[n])
        pieces = jnp.concatenate([raw[x, z] for x in range(4)], axis=0)
        block(z)[...] = mm(ordering, pieces).astype(BF16).reshape(4, 48, OWN)
        put(block(z), block(z), c_send.at[n], c_recv, other)

    own_piece = raw.at[me.x, me.z]
    done(own_piece, m_recv)
    put(own_piece, own_piece, f_send.at[0], f_recv.at[0], z_up)
    put(own_piece, own_piece, b_send.at[0], b_recv.at[0], z_down)
    share(0)

    len_out[...] = jnp.full((8, 128), lens[0], I32)
    eye = (iota((ROWS, ROWS), 0) == iota((ROWS, ROWS), 1)).astype(BF16)
    lookup = mm_nt(eye, (iota((256, ROWS), 0) == ids[...]).astype(BF16)).astype(BF16)
    done(table, t_sem)
    emb[...] = mm(lookup, table[...]).astype(BF16)

    for k in range(4):
        y = (me.y + k) % 4
        args = (emb, every.at[me.role], e_send.at[k], e_recv.at[me.role],
                me.to(y_hi=y // 2, y_lo=y % 2, core=me.y_hi))
        if k:
            put(*args)
        else:
            put_or_keep(straight, *args)

    put_or_keep(straight, hist, events, hi_send.at[0], hi_recv.at[0], mirror)
    put_or_keep(straight, len_out, len_in, hi_send.at[1], hi_recv.at[1], mirror)

    def slots(shape, dim):
        slot = iota(shape, dim)
        return (slot // 16) * 8 + slot % 8, (slot // 8) % 2

    routes = mm_nt(eye, routes_t[...].astype(BF16)).astype(I32)
    expert, order = slots((128, ROWS), 0)
    named = jnp.logical_or(routes_t[0:1, :] == expert, routes_t[1:2, :] == expert)
    earlier = (iota((ROWS, ROWS), 0) < iota((ROWS, ROWS), 1)).astype(BF16)
    before = mm(named.astype(BF16), earlier)
    placing = jnp.logical_and(named, before == order.astype(F32)).astype(BF16)
    expert_l, order_l = slots((ROWS, 128), 1)
    member = [routes[:, k : k + 1] == expert_l for k in range(2)]
    later = (iota((ROWS, ROWS), 1) < iota((ROWS, ROWS), 0)).astype(BF16)
    before_l = mm(later, jnp.logical_or(member[0], member[1]).astype(BF16))
    taking = [jnp.logical_and(m, before_l == order_l.astype(F32)).astype(BF16) for m in member]

    def lagging(stage, t):
        if t == 0:
            stage(0)
        elif 0 < t < 8:
            stage(t)
            stage(t + 7)
        elif t == 8:
            stage(15)

    for t in range(1, 9 + LAG[1]):
        if t < 9:
            for n, send, recv, to in ((t, f_send, f_recv, z_up), (t + 7, b_send, b_recv, z_down)):
                if t == 8 and n == 8:
                    continue
                ref = raw.at[me.x, z_of(n)]
                done(ref, recv.at[t - 1])
                if t < 7 or (t == 7 and n == 14):
                    put(ref, ref, send.at[t], recv.at[t], to)
                share(n)
        lagging(pass_on, t - LAG[0])
        lagging(settle, t - LAG[1])

    for k in range(4):
        done(every.at[k], e_recv.at[k])
    normed = norm_rows(every[...].reshape(4 * ROWS, D).astype(F32), gain[...].reshape(1, D))
    done(events, hi_recv.at[0])
    done(len_in, hi_recv.at[1])
    half = w.at[:, pl.ds(pl.multiple_of((1 - me.core) * 768, 16), 768), :]
    done(half, c_recv)

    keys = mm(events[...], w[0]).astype(BF16)
    values = mm(events[...], w[1]).astype(BF16)
    queries = mm(normed, w[2]).astype(BF16)
    visible = iota((128, 128), 1) < len_in[0:1, :]
    low = iota((128, 128), 1) < HEAD
    mixed = []
    for pair in range(OWN // 128):
        cols = slice(128 * pair, 128 * pair + 128)
        q, k, v = queries[:, cols], keys[:, cols], values[:, cols]
        outs = []
        for mask in (low, jnp.logical_not(low)):
            scores = mm_nt(jnp.where(mask, q, jnp.zeros_like(q)), k) * HEAD ** -0.5
            scores = jnp.where(visible, scores, -1e30)
            weights = jnp.exp(scores - jnp.max(scores, axis=-1, keepdims=True))
            probs = (weights / jnp.sum(weights, axis=-1, keepdims=True)).astype(BF16)
            outs.append(mm(probs, v))
        mixed.append(jnp.where(low, outs[0], outs[1]).astype(BF16))
    mixed = jnp.concatenate(mixed, axis=1)
    part[...] = mm_nt(mixed, w[3]).astype(BF16).reshape(4, ROWS, D)

    for level in range(4):
        own = jnp.logical_and(straight, me.role == level)
        put_or_keep(own, part.at[level], parts.at[me.y], o_send.at[level], o_recv.at[me.y],
                    me.to(y_hi=me.core, y_lo=level // 2, core=level % 2))
    for k in range(4):
        done(parts.at[k], o_recv.at[k])
    attended = parts[0].astype(F32) + parts[1].astype(F32) + parts[2].astype(F32) + parts[3].astype(F32)
    hidden = (emb[...].astype(F32) + attended).astype(BF16).astype(F32)
    moe_in = norm_rows(hidden, moe_gain[...].reshape(1, D))
    packed[...] = mm(placing, moe_in).astype(BF16)

    def cut(ref, k):
        return ref.at[pl.ds(pl.multiple_of(k * 16, 16), 16), :]

    pltpu.make_async_copy(cut(packed, col), cut(got_y, col), y_recv.at[col]).start()
    for k in range(1, 8):
        d = (col + k) % 8
        put(cut(packed, d), cut(got_y, col), y_send.at[k], y_recv.at[col], in_column(d))

    logits = mm_nt(moe_in, router_t[...])
    lanes = iota(logits.shape, 1)
    picked = [
        jnp.sum(jnp.where(routes[:, k : k + 1] == lanes, logits, 0.0), axis=-1, keepdims=True)
        for k in range(2)
    ]
    top = jnp.maximum(picked[0], picked[1])
    powers = [jnp.exp(p - top) for p in picked]
    gates = [p / (powers[0] + powers[1]) for p in powers]

    all_left(but_last=7)
    for k in range(8):
        done(cut(got_y, k), y_recv.at[k])
    o, i = iota((128, 128), 0), iota((128, 128), 1)
    source = ((o // 2) % 8) * 16 + (o % 2) * 8 + o // 16
    sorted_z[...] = mm((source == i).astype(BF16), got_y[...]).astype(BF16)

    def send_z():
        own = rows.at[0, me.x, z_lo]
        pltpu.make_async_copy(cut(sorted_z, zp), own, z_recv.at[0]).start()
        for n in Z_ORDER:
            if n:
                for first, p, s in ((0, (zp + n) % 8, 1 - z_lo), (1, (zp + 8 - n) % 8, z_lo)):
                    put(cut(sorted_z, p), rows.at[2 * n + s, me.x, first],
                        z_send.at[2 * n + first], z_recv.at[2 * n + s], me.to(z=p * 2 + first))
            else:
                p = (zp + 4) % 8
                put(cut(sorted_z, p), rows.at[1, me.x, 1 - z_lo], z_send.at[1], z_recv.at[1], me.to(z=p * 2 + 1 - z_lo))

    def share_own(q):
        mine = rows.at[q, me.x, z_lo]
        done(mine, z_recv.at[q])
        put(mine, mine, p_send.at[q], p_recv.at[q], mate)
        put(mine, mine, g_send.at[q, 0, z_lo], g_recv.at[q, 0, z_lo], up)
        put(mine, mine, g_send.at[q, 1, z_lo], g_recv.at[q, 1, z_lo], down)

    def share_mate(q):
        theirs = rows.at[q, me.x, 1 - z_lo]
        done(theirs, p_recv.at[q])
        put(theirs, theirs, g_send.at[q, 0, 1 - z_lo], g_recv.at[q, 0, 1 - z_lo], up)
        put(theirs, theirs, g_send.at[q, 1, 1 - z_lo], g_recv.at[q, 1, 1 - z_lo], down)

    def relay(q):
        first, second = rows.at[q, x_down, 0], rows.at[q, x_up, 1]
        done(first, g_recv.at[q, 0, 0])
        put(first, first, r_send.at[q, 0], r_recv.at[q, 0], up)
        done(second, g_recv.at[q, 1, 1])
        put(second, second, r_send.at[q, 1], r_recv.at[q, 1], down)
        done(rows.at[q, x_down, 1], g_recv.at[q, 0, 1])
        done(rows.at[q, x_up, 0], g_recv.at[q, 1, 0])

    def apply(q):
        for b in range(2):
            done(rows.at[q, x_far, b], r_recv.at[q, b])
        if q == ORDER[0]:
            for k, dst in enumerate((wg, wu, wd)):
                done(dst, w_sem.at[k])
        here = rows[q].reshape(128, D)
        gate, lift = mm(here, wg[...]), mm(here, wu[...])
        inner = (gate / (1.0 + jnp.exp(-gate)) * lift).astype(BF16)
        res[q] = mm(inner, wd[...]).astype(BF16).reshape(4, 2, 16, D)
        put(res.at[q, x_far, 0], halves.at[q, 0], h_send.at[q, 0], h_recv.at[q, 0], up)
        put(res.at[q, x_far, 1], halves.at[q, 1], h_send.at[q, 1], h_recv.at[q, 1], down)

    def add_halves(q):
        for b, x, to in ((0, x_up, up), (1, x_down, down)):
            done(halves.at[q, b], h_recv.at[q, b])
            res[q, x, b] = (res[q, x, b].astype(F32) + halves[q, b].astype(F32)).astype(BF16)
            put(res.at[q, x], sums.at[q, b], s_send.at[q, b], s_recv.at[q, b], to)

    def total(q, z):
        return res[q, me.x, z].astype(F32) + sums[q, 0, z].astype(F32) + sums[q, 1, z].astype(F32)

    def add_x(q):
        for b in range(2):
            done(sums.at[q, b], s_recv.at[q, b])
        z_out[q] = total(q, 1 - z_lo).astype(BF16)
        put(z_out.at[q], z_in.at[q], q_send.at[q], q_recv.at[q], mate)

    def add_mate(q):
        done(z_in.at[q], q_recv.at[q])
        fin[q] = (total(q, z_lo) + z_in[q].astype(F32)).astype(BF16)
        n, s = q // 2, q % 2
        if n:
            p = (zp + 8 - n + 2 * n * z_lo) % 8
            to = me.to(z=p * 2 + (1 - s) * (1 - z_lo) + s * z_lo)
            put(fin.at[q], cut(back_z, zp), bz_send.at[q], bz_recv.at[2 * n + z_lo], to)
        elif s:
            p = (zp + 4) % 8
            put(fin.at[1], cut(back_z, zp), bz_send.at[1], bz_recv.at[1], me.to(z=p * 2 + 1 - z_lo))
        else:
            pltpu.make_async_copy(fin.at[0], cut(back_z, zp), bz_recv.at[0]).start()

    def run(stages):
        for tick in range(CHUNKS + max(begin for _, begin in stages)):
            for stage, begin in stages:
                if 0 <= tick - begin < CHUNKS:
                    stage(ORDER[tick - begin])

    send_z()
    run(list(zip((share_own, share_mate, relay, apply, add_halves, add_x, add_mate), BEGIN)))

    for n in range(4):
        if n:
            done(cut(back_z, (zp + n) % 8), bz_recv.at[2 * n])
            done(cut(back_z, (zp + 8 - n) % 8), bz_recv.at[2 * n + 1])
        else:
            done(cut(back_z, zp), bz_recv.at[0])
            done(cut(back_z, (zp + 4) % 8), bz_recv.at[1])
    source = (o % 8) * 16 + (o // 16) * 2 + (o // 8) % 2
    sorted_y[...] = mm((source == i).astype(BF16), back_z[...]).astype(BF16)
    pltpu.make_async_copy(cut(sorted_y, col), cut(back_y, col), by_recv.at[col]).start()
    for k in range(1, 8):
        d = (col + k) % 8
        put(cut(sorted_y, d), cut(back_y, col), by_send.at[k], by_recv.at[col], in_column(d))
    all_left(but_last=7)
    for k in range(8):
        done(cut(back_y, k), by_recv.at[k])

    chosen = gates[0] * mm(taking[0], back_y[...]) + gates[1] * mm(taking[1], back_y[...])
    out[...] = (hidden + chosen).astype(BF16)

    all_left()


def dma(*shape):
    return pltpu.SemaphoreType.DMA(shape)


def vmem(*shape, dtype=BF16):
    return pltpu.VMEM(shape, dtype)


VM = pl.BlockSpec(memory_space=pltpu.VMEM)
SM = pl.BlockSpec(memory_space=pltpu.SMEM)
HB = pl.BlockSpec(memory_space=pltpu.HBM)
ONE = pltpu.SemaphoreType.DMA


def shards(history, lengths, beam_ids, routes, code_table, w_key, w_value, w_query, w_out,
           norm_gain, moe_gain, w_router, w_gate, w_up, w_down):
    n = CHUNKS
    result = pl.pallas_call(
        layer_kernel,
        out_shape=jax.ShapeDtypeStruct((ROWS, D), BF16),
        in_specs=[VM, SM] + [VM] * 8 + [HB] * 5,
        out_specs=VM,
        scratch_shapes=[
            vmem(256, D), vmem(ROWS, D), vmem(4, ROWS, D), vmem(128, D),
            vmem(8, 128, dtype=I32), vmem(8, 128, dtype=I32),
            vmem(48, OWN), vmem(4, 16, 48, OWN), vmem(4, D, OWN), vmem(4, ROWS, D), vmem(4, ROWS, D),
            vmem(D, OWN), vmem(D, OWN), vmem(OWN, D), vmem(128, D), vmem(128, D), vmem(128, D),
            vmem(n, 4, 2, 16, D), vmem(n, 4, 2, 16, D), vmem(n, 2, 16, D), vmem(n, 2, 2, 16, D),
            vmem(n, 16, D), vmem(n, 16, D), vmem(n, 16, D), vmem(128, D), vmem(128, D), vmem(128, D),
            ONE, dma(3), ONE, ONE, dma(4), dma(4), dma(2), dma(2),
            dma(8), dma(8), dma(8), dma(8), dma(16, 2), dma(16, 2), dma(16), dma(16), dma(16), ONE, dma(4), dma(4),
            dma(8), dma(8), dma(n), dma(n), dma(n), dma(n), dma(n, 2, 2), dma(n, 2, 2), dma(n, 2), dma(n, 2),
            dma(n, 2), dma(n, 2), dma(n, 2), dma(n, 2), dma(n), dma(n), dma(n), dma(n), dma(8), dma(8),
        ],
        compiler_params=pltpu.CompilerParams(
            collective_id=0, has_side_effects=True, vmem_limit_bytes=56 * 1024 * 1024
        ),
        name="layer",
    )(beam_ids.reshape(1, ROWS), lengths, routes.reshape(ROWS, 2).T, norm_gain, moe_gain,
      w_key, w_value, w_query, w_out.T, w_router.T, code_table, history[0], w_gate[0], w_up[0], w_down[0])
    return result.reshape(1, 1, ROWS, D)


def solution(mesh):
    return jax.shard_map(
        shards,
        mesh=mesh,
        in_specs=(
            P("shard", None, None),
            P("shard"),
            P("shard", "role", None),
            P("shard", "role", None, None),
            P("role", None),
            P("shard", "role"),
            P("shard", "role"),
            P("shard", "role"),
            P("role", "shard"),
            P(),
            P(),
            P(),
            P(("role", "shard"), None, None),
            P(("role", "shard"), None, None),
            P(("role", "shard"), None, None),
        ),
        out_specs=P("shard", "role", None, None),
        check_vma=False,
    )
```
